256 devices in a mesh: ctx: 64 (over x, y, z_hi, core), tp: 4 (over z_lo).
Axes of the slice: x: 4, y: 4, z: 8 (z_hi: 2, z_lo: 4; z = z_hi * 4 + z_lo), core: 2. Of those that a mesh axis runs over, the one named last changes fastest.
Arguments:
- query_rows: bfloat16 [8192, 2048], P('ctx', 'tp'), may hold values from -16 to 16
- key_rows: bfloat16 [8192, 2048], P('ctx', 'tp'), may hold values from -6 to 6
- value_rows: bfloat16 [8192, 2048], P('ctx', 'tp'), may hold values from -6 to 6
- long_filter: float32 [8192, 2048], P('ctx', 'tp'), may hold values from -24 to 24
- out_weight: bfloat16 [2048, 4096], P(None, 'tp'), may hold values from -0.125 to 0.125
- grad_out: bfloat16 [8192, 4096], P('ctx', 'tp'), may hold values from -1.5 to 1.5
Outputs:
- output: bfloat16 [8192, 4096], P('ctx', 'tp')
- grad_query: bfloat16 [8192, 2048], P('ctx', 'tp')
- grad_key: bfloat16 [8192, 2048], P('ctx', 'tp')
- grad_value: bfloat16 [8192, 2048], P('ctx', 'tp')
- grad_filter: float32 [8192, 2048], P('ctx', 'tp')
- grad_weight: float32 [2048, 4096], P('ctx', 'tp')
The draws below stay inside these ranges and needn't reach their ends.
All inputs are finite; a program needn't handle non-finite values.
Results may differ from the reference program's by a relative error of at most 0.0049.
Values may be sent and summed in bfloat16 or wider, within the bound.
A program may use at most 128 MiB of HBM per device.

```python
import math
import jax
import jax.numpy as jnp

D = 4096
C = 2048
SEQ = 8192


def draw_long_filter(key, part):
    key = jax.random.fold_in(key, 7)
    pick_key, slow_key, fast_key, noise_key, gain_key = jax.random.split(key, 5)
    positions = jnp.arange(SEQ, dtype=jnp.float32)[:, None]
    slow_share = 0.5
    noise_part = jnp.clip(jax.random.normal(noise_key, (SEQ, C)), -6.0, 6.0)
    channel_gains = jnp.exp(jax.random.uniform(gain_key, (C,), minval=math.log(0.5), maxval=math.log(2.0)))
    slow_rates = jnp.exp(jax.random.uniform(slow_key, (C,), minval=math.log(0.1 / SEQ), maxval=math.log(2.0 / SEQ)))
    fast_rates = jnp.exp(jax.random.uniform(fast_key, (C,), minval=math.log(2.0 / SEQ), maxval=math.log(1.0 / 30.0)))
    chosen = jax.random.uniform(pick_key, (C,)) < slow_share
    decay_rates = jnp.where(chosen, slow_rates, fast_rates)
    energy = jnp.expm1(-2.0 * decay_rates * SEQ) / jnp.expm1(-2.0 * decay_rates)
    return (noise_part * jnp.exp(-decay_rates * positions) * channel_gains / jnp.sqrt(energy)).astype(jnp.float32)


def raised(array, stream_key, source, target, shards_of, factor):
    def block_of(dim):
        return (jnp.arange(array.shape[dim]) // (array.shape[dim] // shards_of)).reshape((-1,) + (1,) * (array.ndim - 1 - dim))

    near = jax.random.permutation(stream_key, shards_of)[block_of(target)]
    other_side = (block_of(target) + shards_of // 2) % shards_of
    return jnp.where((block_of(source) == near) | (block_of(source) == other_side), factor * array, array)


def shard_levels(own_key, extent, cuts, least, high):
    def one(axis_at, parts):
        steps = jax.random.uniform(jax.random.fold_in(jax.random.fold_in(own_key, 6), axis_at), (parts,), jnp.float32, least / len(cuts), high / len(cuts))
        return jnp.repeat(jnp.exp(steps), extent[axis_at] // parts).reshape((-1,) + (1,) * (len(extent) - axis_at - 1))

    level = one(*cuts[0])
    for cut in cuts[1:]:
        level = level * one(*cut)
    return level


def bell_draw(key, dims, deviation, bound, cuts=(), kind=jnp.bfloat16):
    drawn = jax.random.normal(key, dims, jnp.float32) * deviation
    if len(cuts) > 0:
        drawn = shard_levels(key, dims, cuts, -0.22, 0.18) * drawn
    return jnp.clip(drawn, min=-bound, max=bound).astype(kind)


def noise_with(key, shape, width, bound, cuts, heavy, kind=jnp.bfloat16):
    drawn = width * jax.random.normal(key, shape, jnp.float32)
    if cuts:
        drawn = drawn * shard_levels(key, shape, cuts, -0.22, 0.18)
    return jnp.clip(raised(drawn, jax.random.fold_in(key, 3), *heavy), -bound, bound).astype(kind)


def setup_inputs(seed: int = 0) -> dict:
    streams_of = jax.random.split(jax.random.key(seed), 7)
    query_rows = noise_with(streams_of[0], (SEQ, C), 1.0, 16.0, ((0, 64), (1, 4)), (0, 1, 64, 4.0))
    key_rows = bell_draw(streams_of[1], (SEQ, C), 1.0, 6.0, ((0, 64), (1, 4)))
    value_rows = bell_draw(streams_of[2], (SEQ, C), 1.0, 6.0, ((0, 64), (1, 4)))
    long_filter = draw_long_filter(jax.random.fold_in(streams_of[6], 71), 0)
    out_weight = bell_draw(streams_of[4], (C, D), C ** -0.5, 0.125, ((1, 4),))
    grad_out = bell_draw(streams_of[5], (SEQ, D), 0.25, 1.5, ((0, 64), (1, 4)))
    return {"query_rows": query_rows, "key_rows": key_rows, "value_rows": value_rows, "long_filter": long_filter, "out_weight": out_weight, "grad_out": grad_out}


def causal_conv(gated_input, filter_rows):
    length = gated_input.shape[0]
    spectrum = jnp.fft.rfft(gated_input, n=2 * length, axis=0) * jnp.fft.rfft(filter_rows, n=2 * length, axis=0)
    return jnp.fft.irfft(spectrum, n=2 * length, axis=0)[:length]

def reference(query_rows, key_rows, value_rows, long_filter, out_weight, grad_out):
    query_float = query_rows.astype(jnp.float32)
    key_float = key_rows.astype(jnp.float32)
    value_float = value_rows.astype(jnp.float32)
    gated_input = key_float * value_float
    convolved, pullback = jax.vjp(causal_conv, gated_input, long_filter)
    mixed_rows = (query_float * convolved).astype(jnp.bfloat16)
    output = jnp.dot(mixed_rows, out_weight, preferred_element_type=jnp.float32).astype(jnp.bfloat16)
    grad_mixed = jnp.dot(grad_out, out_weight.T, preferred_element_type=jnp.float32)
    grad_query = (grad_mixed * convolved).astype(jnp.bfloat16)
    grad_conv = grad_mixed * query_float
    grad_gated, grad_filter = pullback(grad_conv)
    grad_key = (grad_gated * value_float).astype(jnp.bfloat16)
    grad_value = (grad_gated * key_float).astype(jnp.bfloat16)
    grad_weight = jnp.dot(mixed_rows.T, grad_out, preferred_element_type=jnp.float32)
    return (output, grad_query, grad_key, grad_value, grad_filter, grad_weight)
```

```python
import functools

import jax
import jax.numpy as jnp
from jax import lax
from jax.experimental import pallas as pl
from jax.experimental.pallas import tpu as pltpu
from jax.sharding import PartitionSpec as P

f32 = jnp.float32
bf16 = jnp.bfloat16
MESH = pl.DeviceIdType.MESH
OWN = 8
TOK = 128


def dot_nn(a, b):
    return lax.dot_general(a, b, (((1,), (0,)), ((), ())), preferred_element_type=f32)


def dot_nt(a, b):
    return lax.dot_general(a, b, (((1,), (1,)), ((), ())), preferred_element_type=f32)


def kernel(
    dims,
    q_ref,
    k_ref,
    v_ref,
    f_ref,
    w_ref,
    go_ref,
    out_ref,
    gq_ref,
    gk_ref,
    gv_ref,
    gf_ref,
    gw_ref,
    s1_ref,
    r1_ref,
    xf_ref,
    xpad_ref,
    gpad_ref,
    t_ref,
    qt_ref,
    gm_ref,
    ps_ref,
    pr_ref,
    gs_ref,
    gr_ref,
    ys_ref,
    yr_ref,
    pqf_ref,
    pqs_ref,
    pqr_ref,
    mix_ref,
    b_ref,
    a_ref,
    cf_ref,
    cs_ref,
    cr_ref,
    zs_ref,
    zr_ref,
    send_sem,
    recv_sem,
    tp_send,
    tp_recv,
    mx_send,
    mx_recv,
):
    nx, ny, nz, nc, nt = dims
    n = nx * ny * nz * nc
    ch = OWN * n
    cols = go_ref.shape[1]
    gwr = gw_ref.shape[0]
    group = nx * nc
    me = lax.axis_index("ctx")
    tp = lax.axis_index("tp")
    core = me % nc
    zh = me // nc % nz
    yy = me // (nc * nz) % ny
    xx = me // (nc * nz * ny)
    slot = xx * nc + core

    row_id = lax.broadcasted_iota(jnp.int32, (TOK, TOK), 0)
    col_id = lax.broadcasted_iota(jnp.int32, (TOK, TOK), 1)
    eye = (row_id == col_id).astype(f32).astype(bf16)
    rev = (row_id + col_id == TOK - 1).astype(f32).astype(bf16)
    lower = col_id >= row_id

    def remote(src, dst, ssem, rsem, device):
        return pltpu.make_async_remote_copy(
            src_ref=src,
            dst_ref=dst,
            send_sem=ssem,
            recv_sem=rsem,
            device_id=device,
            device_id_type=MESH,
        )

    def wait_rows(ref, rows, sem):
        pltpu.make_async_copy(ref.at[pl.ds(0, rows)], ref.at[pl.ds(0, rows)], sem).wait()

    def spread(src, dst, size, src_block, dst_block, index):
        def one(step, carry):
            peer = (me + step) % n
            remote(
                src.at[pl.ds(pl.multiple_of(src_block(peer) * size, size), size)],
                dst.at[pl.ds(pl.multiple_of(dst_block * size, size), size)],
                send_sem.at[index],
                recv_sem.at[index],
                {"ctx": peer},
            ).start()
            return carry

        lax.fori_loop(1, n, one, 0)

    barrier = pltpu.get_barrier_semaphore()

    def greet(step, carry):
        pl.semaphore_signal(
            barrier, inc=1, device_id={"ctx": (me + step) % n}, device_id_type=MESH
        )
        return carry

    lax.fori_loop(1, n, greet, 0)
    for step in range(1, nt):
        pl.semaphore_signal(
            barrier, inc=1, device_id={"tp": (tp + step) % nt}, device_id_type=MESH
        )

    for j in range(ch // TOK):
        lanes = pl.ds(j * TOK, TOK)
        gated = (k_ref[:, lanes].astype(f32) * v_ref[:, lanes].astype(f32)).astype(bf16)
        gated_t = dot_nt(eye, gated).reshape(TOK // OWN, OWN, TOK)
        filter_t = dot_nt(eye, f_ref[:, lanes].astype(bf16)).reshape(TOK // OWN, OWN, TOK)
        both = jnp.concatenate([gated_t, filter_t], axis=1)
        s1_ref[pl.ds(2 * j * TOK, 2 * TOK), :] = both.reshape(2 * TOK, TOK).astype(bf16)
        qt_ref[pl.ds(j * TOK, TOK), :] = dot_nt(eye, q_ref[:, lanes])

    pl.semaphore_wait(barrier, n - 1 + nt - 1)
    spread(s1_ref, r1_ref, 2 * OWN, lambda peer: peer, me, 0)

    part = min(ch, 256)

    def partial(target, write):
        def rows(i, carry):
            start = pl.multiple_of(target * ch + i * part, part)
            write(
                pl.ds(pl.multiple_of(i * part, part), part),
                dot_nt(w_ref[pl.ds(start, part), :], go_ref[...]),
            )
            return carry

        lax.fori_loop(0, ch // part, rows, 0)

    for step in range(1, nt):
        peer = (tp + step) % nt

        def put(rows, value, step=step):
            ps_ref[step - 1, rows, :] = value.astype(bf16)

        partial(peer, put)
        remote(
            ps_ref.at[step - 1],
            pr_ref.at[step - 1],
            tp_send.at[step - 1],
            tp_recv.at[step - 1],
            {"tp": peer},
        ).start()

    def put_own(rows, value):
        gm_ref[rows, :] = value

    partial(tp, put_own)

    def share(step, carry):
        other = (slot + step) % group
        peer = ((other // nc * ny + yy) * nz + zh) * nc + other % nc
        remote(go_ref, b_ref.at[slot], send_sem.at[4], recv_sem.at[4], {"ctx": peer}).start()
        return carry

    lax.fori_loop(1, group, share, 0)

    for step in range(1, nt):
        remote(
            ps_ref.at[step - 1],
            pr_ref.at[step - 1],
            tp_send.at[step - 1],
            tp_recv.at[step - 1],
            {"tp": (tp + step) % nt},
        ).wait_recv()

    def sum_rows(i, carry):
        rows = pl.ds(pl.multiple_of(i * TOK, TOK), TOK)
        total = gm_ref[rows, :]
        for step in range(1, nt):
            total = total + pr_ref[step - 1, rows, :].astype(f32)
        gm_ref[rows, :] = total
        gs_ref[rows, :] = dot_nn((total * qt_ref[rows, :]).astype(bf16), rev)
        return carry

    lax.fori_loop(0, ch // TOK, sum_rows, 0)
    spread(gs_ref, gr_ref, OWN, lambda peer: peer, n - 1 - me, 1)

    wait_rows(r1_ref, (n - 1) * 2 * OWN, recv_sem.at[0])
    mine = pl.ds(pl.multiple_of(me * 2 * OWN, 2 * OWN), 2 * OWN)
    r1_ref[mine, :] = s1_ref[mine, :]
    xf_ref[...] = r1_ref[...].astype(f32)

    def toeplitz(c, first, lanes):
        def block(d, before):
            line = xf_ref[pl.ds(d * 2 * OWN + first + c, 1), :]
            now = pltpu.roll(
                jnp.broadcast_to(line, (TOK, TOK)), 0, 1, stride=1, stride_axis=0
            )
            t_ref[c, d, :, lanes] = jnp.where(lower, now, before).astype(bf16)
            return now

        lax.fori_loop(0, n, block, jnp.zeros((TOK, TOK), f32))

    def convolve(pad, c, lanes, width):
        def step(e, acc):
            left = jnp.concatenate(
                [pad[c, pl.ds(n - 2 * e, n), :], pad[c, pl.ds(n - 1 - 2 * e, n), :]], axis=1
            ).astype(bf16)
            right = t_ref[c, pl.ds(2 * e, 2), :, lanes].reshape(2 * TOK, width)
            return acc + dot_nn(left, right)

        return lax.fori_loop(0, n // 2, step, jnp.zeros((n, width), f32))

    def forward(c, carry):
        xpad_ref[c, pl.ds(0, n), :] = jnp.zeros((n, TOK), f32)
        xpad_ref[c, pl.ds(n, n), :] = xf_ref[pl.ds(c, n, stride=2 * OWN), :]
        toeplitz(c, OWN, pl.ds(0, TOK))
        ys_ref[pl.ds(c, n, stride=OWN), :] = convolve(xpad_ref, c, pl.ds(0, TOK), TOK)
        return carry

    lax.fori_loop(0, OWN, forward, 0)
    spread(ys_ref, yr_ref, OWN, lambda peer: peer, me, 2)

    def other_blocks(c, carry):
        toeplitz(c, 0, pl.ds(TOK, TOK))
        return carry

    lax.fori_loop(0, OWN, other_blocks, 0)

    wait_rows(yr_ref, (n - 1) * OWN, recv_sem.at[2])
    mine8 = pl.ds(pl.multiple_of(me * OWN, OWN), OWN)
    yr_ref[mine8, :] = ys_ref[mine8, :]
    per = ny * nz * nc * gwr // TOK

    def mix(i, carry):
        rows = pl.ds(pl.multiple_of(i * TOK, TOK), TOK)
        mixed = (qt_ref[rows, :] * yr_ref[rows, :]).astype(bf16)
        mix_ref[pl.ds(pl.multiple_of(tp * ch + i * TOK, TOK), TOK), :] = mixed
        return carry

    lax.fori_loop(0, ch // TOK, mix, 0)
    own_rows = pl.ds(pl.multiple_of(tp * ch, ch), ch)
    for step in range(1, nt):
        remote(
            mix_ref.at[own_rows],
            mix_ref.at[own_rows],
            mx_send.at[step - 1],
            mx_recv.at[step - 1],
            {"tp": (tp + step) % nt},
        ).start()

    wait_rows(gr_ref, (n - 1) * OWN, recv_sem.at[1])
    gr_ref[pl.ds(pl.multiple_of((n - 1 - me) * OWN, OWN), OWN), :] = gs_ref[mine8, :]

    def backward(c, carry):
        gpad_ref[c, pl.ds(0, n), :] = jnp.zeros((n, TOK), f32)
        gpad_ref[c, pl.ds(n, n), :] = gr_ref[pl.ds(c, n, stride=OWN), :]
        acc = convolve(gpad_ref, c, pl.ds(0, 2 * TOK), 2 * TOK)
        pqf_ref[pl.ds(c, n, stride=2 * OWN), :] = acc[:, :TOK]
        pqf_ref[pl.ds(OWN + c, n, stride=2 * OWN), :] = acc[:, TOK:]
        return carry

    lax.fori_loop(0, OWN, backward, 0)
    pqs_ref[...] = pqf_ref[...].astype(bf16)
    spread(pqs_ref, pqr_ref, 2 * OWN, lambda peer: n - 1 - peer, me, 3)

    for step in range(1, nt):
        source = (tp + nt - step) % nt
        rows = pl.ds(pl.multiple_of(source * ch, ch), ch)
        remote(
            mix_ref.at[rows],
            mix_ref.at[rows],
            mx_send.at[step - 1],
            mx_recv.at[step - 1],
            {"tp": (tp + step) % nt},
        ).wait_recv()

    blocks = ny * nz

    def block_rows(other, b):
        index = (other // nc * blocks + b) * nc + other % nc
        return pl.ds(pl.multiple_of(index * gwr, gwr), gwr)

    def feed(step, carry):
        other = (slot + step) % group
        peer = ((other // nc * ny + yy) * nz + zh) * nc + other % nc

        def one(b, inner):
            remote(
                mix_ref.at[block_rows(other, b)],
                a_ref.at[slot, pl.ds(pl.multiple_of(b * gwr, gwr), gwr)],
                send_sem.at[5],
                recv_sem.at[5],
                {"ctx": peer},
            ).start()
            return inner

        lax.fori_loop(0, blocks, one, 0)
        return carry

    lax.fori_loop(1, group, feed, 0)

    wide = min(cols, 256)

    def project(i, carry):
        columns = pl.ds(pl.multiple_of(i * wide, wide), wide)
        acc = jnp.zeros((TOK, wide), f32)
        for source in range(nt):
            rows = pl.ds(source * ch, ch)
            left = dot_nt(eye, mix_ref[rows, :]).astype(bf16)
            acc = acc + dot_nn(left, w_ref[rows, columns])
        out_ref[:, columns] = acc.astype(bf16)
        return carry

    lax.fori_loop(0, cols // wide, project, 0)

    wait_rows(b_ref, group - 1, recv_sem.at[4])
    wait_rows(a_ref, group - 1, recv_sem.at[5])
    b_ref[slot] = go_ref[...]

    def keep(b, carry):
        a_ref[slot, pl.ds(pl.multiple_of(b * gwr, gwr), gwr), :] = mix_ref[
            block_rows(slot, b), :
        ]
        return carry

    lax.fori_loop(0, blocks, keep, 0)
    tall = nz * gwr

    def weight(i, carry):
        columns = pl.ds(pl.multiple_of(i * wide, wide), wide)
        acc = jnp.zeros((blocks * gwr, wide), f32)
        for source in range(group):
            acc = acc + dot_nn(a_ref[source], b_ref[source, :, columns])
        cf_ref[:, columns] = acc
        return carry

    lax.fori_loop(0, cols // wide, weight, 0)
    for y_step in range(1, ny):
        other = (yy + y_step) % ny
        rows = pl.ds(pl.multiple_of(other * tall, tall), tall)
        cs_ref[y_step - 1] = cf_ref[rows, :].astype(bf16)
        peer = ((xx * ny + other) * nz + zh) * nc + core
        remote(
            cs_ref.at[y_step - 1],
            cr_ref.at[y_step - 1],
            send_sem.at[6],
            recv_sem.at[6],
            {"ctx": peer},
        ).start()

    def query(j, carry):
        rows = pl.ds(pl.multiple_of(j * TOK, TOK), TOK)
        grad = (gm_ref[rows, :] * yr_ref[rows, :]).astype(bf16)
        gq_ref[:, rows] = dot_nt(eye, grad).astype(bf16)
        return carry

    lax.fori_loop(0, ch // TOK, query, 0)
    wait_rows(pqr_ref, (n - 1) * 2 * OWN, recv_sem.at[3])
    back = pl.ds(pl.multiple_of((n - 1 - me) * 2 * OWN, 2 * OWN), 2 * OWN)
    pqr_ref[mine, :] = pqs_ref[back, :]

    def finish(j, carry):
        lanes = pl.ds(pl.multiple_of(j * TOK, TOK), TOK)
        both = pqr_ref[pl.ds(pl.multiple_of(2 * j * TOK, TOK), 2 * TOK), :].astype(f32)
        both = both.reshape(TOK // OWN, 2 * OWN, TOK)
        grad_gated = dot_nt(rev, both[:, :OWN].reshape(TOK, TOK).astype(bf16))
        gf_ref[:, lanes] = dot_nt(rev, both[:, OWN:].reshape(TOK, TOK).astype(bf16))
        gk_ref[:, lanes] = (grad_gated * v_ref[:, lanes].astype(f32)).astype(bf16)
        gv_ref[:, lanes] = (grad_gated * k_ref[:, lanes].astype(f32)).astype(bf16)
        return carry

    lax.fori_loop(0, ch // TOK, finish, 0)

    wait_rows(cr_ref, ny - 1, recv_sem.at[6])
    own_z = pl.multiple_of(yy * tall + zh * gwr, gwr)
    far = (zh + 1) % nz
    far_total = cf_ref[pl.ds(pl.multiple_of(yy * tall + far * gwr, gwr), gwr), :]
    own_total = cf_ref[pl.ds(own_z, gwr), :]
    for y_step in range(1, ny):
        far_total = far_total + cr_ref[
            y_step - 1, pl.ds(pl.multiple_of(far * gwr, gwr), gwr), :
        ].astype(f32)
        own_total = own_total + cr_ref[
            y_step - 1, pl.ds(pl.multiple_of(zh * gwr, gwr), gwr), :
        ].astype(f32)
    zs_ref[...] = far_total.astype(bf16)
    gw_ref[...] = own_total
    across = remote(
        zs_ref,
        zr_ref,
        send_sem.at[7],
        recv_sem.at[7],
        {"ctx": ((xx * ny + yy) * nz + far) * nc + core},
    )
    across.start()
    across.wait_recv()
    gw_ref[...] += zr_ref[...].astype(f32)

    wait_rows(s1_ref, (n - 1) * 2 * OWN, send_sem.at[0])
    wait_rows(gs_ref, (n - 1) * OWN, send_sem.at[1])
    wait_rows(ys_ref, (n - 1) * OWN, send_sem.at[2])
    wait_rows(pqs_ref, (n - 1) * 2 * OWN, send_sem.at[3])
    wait_rows(b_ref, group - 1, send_sem.at[4])
    wait_rows(a_ref, group - 1, send_sem.at[5])
    wait_rows(cs_ref, ny - 1, send_sem.at[6])
    across.wait_send()
    for step in range(1, nt):
        peer = {"tp": (tp + step) % nt}
        remote(
            ps_ref.at[step - 1],
            pr_ref.at[step - 1],
            tp_send.at[step - 1],
            tp_recv.at[step - 1],
            peer,
        ).wait_send()
        remote(
            mix_ref.at[own_rows],
            mix_ref.at[own_rows],
            mx_send.at[step - 1],
            mx_recv.at[step - 1],
            peer,
        ).wait_send()


def per_device(dims, q, k, v, f, w, go):
    nx, ny, nz, nc, nt = dims
    n = nx * ny * nz * nc
    ch = OWN * n
    every = ch * nt
    cols = go.shape[1]
    gwr = every // n
    group = nx * nc
    tall = nz * gwr
    vmem = pl.BlockSpec(memory_space=pltpu.VMEM)
    return pl.pallas_call(
        functools.partial(kernel, dims),
        out_shape=(
            jax.ShapeDtypeStruct((TOK, cols), bf16),
            jax.ShapeDtypeStruct((TOK, ch), bf16),
            jax.ShapeDtypeStruct((TOK, ch), bf16),
            jax.ShapeDtypeStruct((TOK, ch), bf16),
            jax.ShapeDtypeStruct((TOK, ch), f32),
            jax.ShapeDtypeStruct((gwr, cols), f32),
        ),
        in_specs=[vmem] * 6,
        out_specs=[vmem] * 6,
        scratch_shapes=[
            pltpu.VMEM((2 * ch, TOK), bf16),
            pltpu.VMEM((2 * ch, TOK), bf16),
            pltpu.VMEM((2 * ch, TOK), f32),
            pltpu.VMEM((OWN, 2 * n, TOK), f32),
            pltpu.VMEM((OWN, 2 * n, TOK), f32),
            pltpu.VMEM((OWN, n, TOK, 2 * TOK), bf16),
            pltpu.VMEM((ch, TOK), f32),
            pltpu.VMEM((ch, TOK), f32),
            pltpu.VMEM((nt - 1, ch, TOK), bf16),
            pltpu.VMEM((nt - 1, ch, TOK), bf16),
            pltpu.VMEM((ch, TOK), f32),
            pltpu.VMEM((ch, TOK), f32),
            pltpu.VMEM((ch, TOK), f32),
            pltpu.VMEM((ch, TOK), f32),
            pltpu.VMEM((2 * ch, TOK), f32),
            pltpu.VMEM((2 * ch, TOK), bf16),
            pltpu.VMEM((2 * ch, TOK), bf16),
            pltpu.VMEM((every, TOK), bf16),
            pltpu.VMEM((group, TOK, cols), bf16),
            pltpu.VMEM((group, ny * nz * gwr, TOK), bf16),
            pltpu.VMEM((ny * nz * gwr, cols), f32),
            pltpu.VMEM((ny - 1, tall, cols), bf16),
            pltpu.VMEM((ny - 1, tall, cols), bf16),
            pltpu.VMEM((gwr, cols), bf16),
            pltpu.VMEM((gwr, cols), bf16),
            pltpu.SemaphoreType.DMA((8,)),
            pltpu.SemaphoreType.DMA((8,)),
            pltpu.SemaphoreType.DMA((nt - 1,)),
            pltpu.SemaphoreType.DMA((nt - 1,)),
            pltpu.SemaphoreType.DMA((nt - 1,)),
            pltpu.SemaphoreType.DMA((nt - 1,)),
        ],
        compiler_params=pltpu.CompilerParams(
            collective_id=0, has_side_effects=True, vmem_limit_bytes=56 * 1024 * 1024
        ),
    )(q, k, v, f, w, go)


def solution(mesh, dims=(4, 4, 2, 2, 4)):
    return jax.shard_map(
        functools.partial(per_device, dims),
        mesh=mesh,
        in_specs=(
            P("ctx", "tp"),
            P("ctx", "tp"),
            P("ctx", "tp"),
            P("ctx", "tp"),
            P(None, "tp"),
            P("ctx", "tp"),
        ),
        out_specs=(P("ctx", "tp"),) * 6,
        check_vma=False,
    )
```

```python
import functools

import jax
import jax.numpy as jnp
from jax import lax
from jax.experimental import pallas as pl
from jax.experimental.pallas import tpu as pltpu
from jax.sharding import PartitionSpec as P

f32 = jnp.float32
bf16 = jnp.bfloat16
MESH = pl.DeviceIdType.MESH
OWN = 8
TOK = 128


def dot_nn(a, b):
    return lax.dot_general(a, b, (((1,), (0,)), ((), ())), preferred_element_type=f32)


def dot_nt(a, b):
    return lax.dot_general(a, b, (((1,), (1,)), ((), ())), preferred_element_type=f32)


def kernel(
    dims,
    q_ref,
    k_ref,
    v_ref,
    f_ref,
    w_ref,
    go_ref,
    out_ref,
    gq_ref,
    gk_ref,
    gv_ref,
    gf_ref,
    gw_ref,
    s1_ref,
    r1_ref,
    xf_ref,
    xpad_ref,
    gpad_ref,
    t_ref,
    qt_ref,
    gm_ref,
    ps_ref,
    pr_ref,
    gs_ref,
    gr_ref,
    ys_ref,
    yr_ref,
    pqf_ref,
    pqs_ref,
    pqr_ref,
    mix_ref,
    b_ref,
    a_ref,
    cf_ref,
    cs_ref,
    cr_ref,
    zs_ref,
    zr_ref,
    send_sem,
    recv_sem,
    tp_send,
    tp_recv,
    mx_send,
    mx_recv,
):
    nx, ny, nz, nc, nt = dims
    n = nx * ny * nz * nc
    ch = OWN * n
    cols = go_ref.shape[1]
    gwr = gw_ref.shape[0]
    group = nx * nc
    me = lax.axis_index("ctx")
    tp = lax.axis_index("tp")
    core = me % nc
    zh = me // nc % nz
    yy = me // (nc * nz) % ny
    xx = me // (nc * nz * ny)
    slot = xx * nc + core

    row_id = lax.broadcasted_iota(jnp.int32, (TOK, TOK), 0)
    col_id = lax.broadcasted_iota(jnp.int32, (TOK, TOK), 1)
    eye = (row_id == col_id).astype(f32).astype(bf16)
    rev = (row_id + col_id == TOK - 1).astype(f32).astype(bf16)
    lower = col_id >= row_id

    def remote(src, dst, ssem, rsem, device):
        return pltpu.make_async_remote_copy(
            src_ref=src,
            dst_ref=dst,
            send_sem=ssem,
            recv_sem=rsem,
            device_id=device,
            device_id_type=MESH,
        )

    def wait_rows(ref, rows, sem):
        pltpu.make_async_copy(ref.at[pl.ds(0, rows)], ref.at[pl.ds(0, rows)], sem).wait()

    def spread(src, dst, size, src_block, dst_block, index):
        def one(step, carry):
            peer = (me + step) % n
            remote(
                src.at[pl.ds(pl.multiple_of(src_block(peer) * size, size), size)],
                dst.at[pl.ds(pl.multiple_of(dst_block * size, size), size)],
                send_sem.at[index],
                recv_sem.at[index],
                {"ctx": peer},
            ).start()
            return carry

        lax.fori_loop(1, n, one, 0)

    barrier = pltpu.get_barrier_semaphore()

    def greet(step, carry):
        pl.semaphore_signal(
            barrier, inc=1, device_id={"ctx": (me + step) % n}, device_id_type=MESH
        )
        return carry

    lax.fori_loop(1, n, greet, 0)
    for step in range(1, nt):
        pl.semaphore_signal(
            barrier, inc=1, device_id={"tp": (tp + step) % nt}, device_id_type=MESH
        )

    for j in range(ch // TOK):
        lanes = pl.ds(j * TOK, TOK)
        gated = (k_ref[:, lanes].astype(f32) * v_ref[:, lanes].astype(f32)).astype(bf16)
        gated_t = dot_nt(eye, gated).reshape(TOK // OWN, OWN, TOK)
        filter_t = dot_nt(eye, f_ref[:, lanes].astype(bf16)).reshape(TOK // OWN, OWN, TOK)
        both = jnp.concatenate([gated_t, filter_t], axis=1)
        s1_ref[pl.ds(2 * j * TOK, 2 * TOK), :] = both.reshape(2 * TOK, TOK).astype(bf16)
        qt_ref[pl.ds(j * TOK, TOK), :] = dot_nt(eye, q_ref[:, lanes])

    pl.semaphore_wait(barrier, n - 1 + nt - 1)
    spread(s1_ref, r1_ref, 2 * OWN, lambda peer: peer, me, 0)

    part = min(ch, 256)

    def partial(target, write):
        def rows(i, carry):
            start = pl.multiple_of(target * ch + i * part, part)
            write(
                pl.ds(pl.multiple_of(i * part, part), part),
                dot_nt(w_ref[pl.ds(start, part), :], go_ref[...]),
            )
            return carry

        lax.fori_loop(0, ch // part, rows, 0)

    for step in range(1, nt):
        peer = (tp + step) % nt

        def put(rows, value, step=step):
            ps_ref[step - 1, rows, :] = value.astype(bf16)

        partial(peer, put)
        remote(
            ps_ref.at[step - 1],
            pr_ref.at[step - 1],
            tp_send.at[step - 1],
            tp_recv.at[step - 1],
            {"tp": peer},
        ).start()

    def put_own(rows, value):
        gm_ref[rows, :] = value

    partial(tp, put_own)

    def share(step, carry):
        other = (slot + step) % group
        peer = ((other // nc * ny + yy) * nz + zh) * nc + other % nc
        remote(go_ref, b_ref.at[slot], send_sem.at[4], recv_sem.at[4], {"ctx": peer}).start()
        return carry

    lax.fori_loop(1, group, share, 0)

    for step in range(1, nt):
        remote(
            ps_ref.at[step - 1],
            pr_ref.at[step - 1],
            tp_send.at[step - 1],
            tp_recv.at[step - 1],
            {"tp": (tp + step) % nt},
        ).wait_recv()

    def sum_rows(i, carry):
        rows = pl.ds(pl.multiple_of(i * TOK, TOK), TOK)
        total = gm_ref[rows, :]
        for step in range(1, nt):
            total = total + pr_ref[step - 1, rows, :].astype(f32)
        gm_ref[rows, :] = total
        gs_ref[rows, :] = dot_nn((total * qt_ref[rows, :]).astype(bf16), rev)
        return carry

    lax.fori_loop(0, ch // TOK, sum_rows, 0)
    spread(gs_ref, gr_ref, OWN, lambda peer: peer, n - 1 - me, 1)

    wait_rows(r1_ref, (n - 1) * 2 * OWN, recv_sem.at[0])
    mine = pl.ds(pl.multiple_of(me * 2 * OWN, 2 * OWN), 2 * OWN)
    r1_ref[mine, :] = s1_ref[mine, :]
    xf_ref[...] = r1_ref[...].astype(f32)

    def toeplitz(c, first, lanes):
        def block(d, before):
            line = xf_ref[pl.ds(d * 2 * OWN + first + c, 1), :]
            now = pltpu.roll(
                jnp.broadcast_to(line, (TOK, TOK)), 0, 1, stride=1, stride_axis=0
            )
            t_ref[c, d, :, lanes] = jnp.where(lower, now, before).astype(bf16)
            return now

        lax.fori_loop(0, n, block, jnp.zeros((TOK, TOK), f32), unroll=min(n, 32))

    def convolve(pad, c, lanes, width):
        left = jnp.concatenate(
            [pad[c, pl.ds(n - i, n), :].astype(bf16) for i in range(n)], axis=1
        )
        return dot_nn(left, t_ref[c, :, :, lanes].reshape(n * TOK, width))

    def forward(c, carry):
        xpad_ref[c, pl.ds(0, n), :] = jnp.zeros((n, TOK), f32)
        xpad_ref[c, pl.ds(n, n), :] = xf_ref[pl.ds(c, n, stride=2 * OWN), :]
        toeplitz(c, OWN, pl.ds(0, TOK))
        ys_ref[pl.ds(c, n, stride=OWN), :] = convolve(xpad_ref, c, pl.ds(0, TOK), TOK)
        return carry

    lax.fori_loop(0, OWN, forward, 0)
    spread(ys_ref, yr_ref, OWN, lambda peer: peer, me, 2)

    def other_blocks(c, carry):
        toeplitz(c, 0, pl.ds(TOK, TOK))
        return carry

    lax.fori_loop(0, OWN, other_blocks, 0)

    wait_rows(yr_ref, (n - 1) * OWN, recv_sem.at[2])
    mine8 = pl.ds(pl.multiple_of(me * OWN, OWN), OWN)
    yr_ref[mine8, :] = ys_ref[mine8, :]
    per = ny * nz * nc * gwr // TOK

    def mix(i, carry):
        rows = pl.ds(pl.multiple_of(i * TOK, TOK), TOK)
        mixed = (qt_ref[rows, :] * yr_ref[rows, :]).astype(bf16)
        mix_ref[pl.ds(pl.multiple_of(tp * ch + i * TOK, TOK), TOK), :] = mixed
        return carry

    lax.fori_loop(0, ch // TOK, mix, 0)
    own_rows = pl.ds(pl.multiple_of(tp * ch, ch), ch)
    for step in range(1, nt):
        remote(
            mix_ref.at[own_rows],
            mix_ref.at[own_rows],
            mx_send.at[step - 1],
            mx_recv.at[step - 1],
            {"tp": (tp + step) % nt},
        ).start()

    wait_rows(gr_ref, (n - 1) * OWN, recv_sem.at[1])
    gr_ref[pl.ds(pl.multiple_of((n - 1 - me) * OWN, OWN), OWN), :] = gs_ref[mine8, :]

    def backward(c, carry):
        gpad_ref[c, pl.ds(0, n), :] = jnp.zeros((n, TOK), f32)
        gpad_ref[c, pl.ds(n, n), :] = gr_ref[pl.ds(c, n, stride=OWN), :]
        acc = convolve(gpad_ref, c, pl.ds(0, 2 * TOK), 2 * TOK)
        pqf_ref[pl.ds(c, n, stride=2 * OWN), :] = acc[:, :TOK]
        pqf_ref[pl.ds(OWN + c, n, stride=2 * OWN), :] = acc[:, TOK:]
        return carry

    lax.fori_loop(0, OWN, backward, 0)
    pqs_ref[...] = pqf_ref[...].astype(bf16)
    spread(pqs_ref, pqr_ref, 2 * OWN, lambda peer: n - 1 - peer, me, 3)

    for step in range(1, nt):
        source = (tp + nt - step) % nt
        rows = pl.ds(pl.multiple_of(source * ch, ch), ch)
        remote(
            mix_ref.at[rows],
            mix_ref.at[rows],
            mx_send.at[step - 1],
            mx_recv.at[step - 1],
            {"tp": (tp + step) % nt},
        ).wait_recv()

    blocks = ny * nz

    def block_rows(other, b):
        index = (other // nc * blocks + b) * nc + other % nc
        return pl.ds(pl.multiple_of(index * gwr, gwr), gwr)

    def feed(step, carry):
        other = (slot + step) % group
        peer = ((other // nc * ny + yy) * nz + zh) * nc + other % nc

        def one(b, inner):
            remote(
                mix_ref.at[block_rows(other, b)],
                a_ref.at[slot, pl.ds(pl.multiple_of(b * gwr, gwr), gwr)],
                send_sem.at[5],
                recv_sem.at[5],
                {"ctx": peer},
            ).start()
            return inner

        lax.fori_loop(0, blocks, one, 0)
        return carry

    lax.fori_loop(1, group, feed, 0)

    wide = min(cols, 256)

    def project(i, carry):
        columns = pl.ds(pl.multiple_of(i * wide, wide), wide)
        acc = jnp.zeros((TOK, wide), f32)
        for source in range(nt):
            rows = pl.ds(source * ch, ch)
            left = dot_nt(eye, mix_ref[rows, :]).astype(bf16)
            acc = acc + dot_nn(left, w_ref[rows, columns])
        out_ref[:, columns] = acc.astype(bf16)
        return carry

    lax.fori_loop(0, cols // wide, project, 0)

    wait_rows(b_ref, group - 1, recv_sem.at[4])
    wait_rows(a_ref, group - 1, recv_sem.at[5])
    b_ref[slot] = go_ref[...]

    def keep(b, carry):
        a_ref[slot, pl.ds(pl.multiple_of(b * gwr, gwr), gwr), :] = mix_ref[
            block_rows(slot, b), :
        ]
        return carry

    lax.fori_loop(0, blocks, keep, 0)
    tall = nz * gwr

    def weight(i, carry):
        columns = pl.ds(pl.multiple_of(i * wide, wide), wide)
        acc = jnp.zeros((blocks * gwr, wide), f32)
        for source in range(group):
            acc = acc + dot_nn(a_ref[source], b_ref[source, :, columns])
        cf_ref[:, columns] = acc
        return carry

    lax.fori_loop(0, cols // wide, weight, 0)
    for y_step in range(1, ny):
        other = (yy + y_step) % ny
        rows = pl.ds(pl.multiple_of(other * tall, tall), tall)
        cs_ref[y_step - 1] = cf_ref[rows, :].astype(bf16)
        peer = ((xx * ny + other) * nz + zh) * nc + core
        remote(
            cs_ref.at[y_step - 1],
            cr_ref.at[y_step - 1],
            send_sem.at[6],
            recv_sem.at[6],
            {"ctx": peer},
        ).start()

    def query(j, carry):
        rows = pl.ds(pl.multiple_of(j * TOK, TOK), TOK)
        grad = (gm_ref[rows, :] * yr_ref[rows, :]).astype(bf16)
        gq_ref[:, rows] = dot_nt(eye, grad).astype(bf16)
        return carry

    lax.fori_loop(0, ch // TOK, query, 0)
    wait_rows(pqr_ref, (n - 1) * 2 * OWN, recv_sem.at[3])
    back = pl.ds(pl.multiple_of((n - 1 - me) * 2 * OWN, 2 * OWN), 2 * OWN)
    pqr_ref[mine, :] = pqs_ref[back, :]

    def finish(j, carry):
        lanes = pl.ds(pl.multiple_of(j * TOK, TOK), TOK)
        both = pqr_ref[pl.ds(pl.multiple_of(2 * j * TOK, TOK), 2 * TOK), :].astype(f32)
        both = both.reshape(TOK // OWN, 2 * OWN, TOK)
        grad_gated = dot_nt(rev, both[:, :OWN].reshape(TOK, TOK).astype(bf16))
        gf_ref[:, lanes] = dot_nt(rev, both[:, OWN:].reshape(TOK, TOK).astype(bf16))
        gk_ref[:, lanes] = (grad_gated * v_ref[:, lanes].astype(f32)).astype(bf16)
        gv_ref[:, lanes] = (grad_gated * k_ref[:, lanes].astype(f32)).astype(bf16)
        return carry

    lax.fori_loop(0, ch // TOK, finish, 0)

    wait_rows(cr_ref, ny - 1, recv_sem.at[6])
    own_z = pl.multiple_of(yy * tall + zh * gwr, gwr)
    far = (zh + 1) % nz
    far_total = cf_ref[pl.ds(pl.multiple_of(yy * tall + far * gwr, gwr), gwr), :]
    own_total = cf_ref[pl.ds(own_z, gwr), :]
    for y_step in range(1, ny):
        far_total = far_total + cr_ref[
            y_step - 1, pl.ds(pl.multiple_of(far * gwr, gwr), gwr), :
        ].astype(f32)
        own_total = own_total + cr_ref[
            y_step - 1, pl.ds(pl.multiple_of(zh * gwr, gwr), gwr), :
        ].astype(f32)
    zs_ref[...] = far_total.astype(bf16)
    gw_ref[...] = own_total
    across = remote(
        zs_ref,
        zr_ref,
        send_sem.at[7],
        recv_sem.at[7],
        {"ctx": ((xx * ny + yy) * nz + far) * nc + core},
    )
    across.start()
    across.wait_recv()
    gw_ref[...] += zr_ref[...].astype(f32)

    wait_rows(s1_ref, (n - 1) * 2 * OWN, send_sem.at[0])
    wait_rows(gs_ref, (n - 1) * OWN, send_sem.at[1])
    wait_rows(ys_ref, (n - 1) * OWN, send_sem.at[2])
    wait_rows(pqs_ref, (n - 1) * 2 * OWN, send_sem.at[3])
    wait_rows(b_ref, group - 1, send_sem.at[4])
    wait_rows(a_ref, group - 1, send_sem.at[5])
    wait_rows(cs_ref, ny - 1, send_sem.at[6])
    across.wait_send()
    for step in range(1, nt):
        peer = {"tp": (tp + step) % nt}
        remote(
            ps_ref.at[step - 1],
            pr_ref.at[step - 1],
            tp_send.at[step - 1],
            tp_recv.at[step - 1],
            peer,
        ).wait_send()
        remote(
            mix_ref.at[own_rows],
            mix_ref.at[own_rows],
            mx_send.at[step - 1],
            mx_recv.at[step - 1],
            peer,
        ).wait_send()


def per_device(dims, q, k, v, f, w, go):
    nx, ny, nz, nc, nt = dims
    n = nx * ny * nz * nc
    ch = OWN * n
    every = ch * nt
    cols = go.shape[1]
    gwr = every // n
    group = nx * nc
    tall = nz * gwr
    vmem = pl.BlockSpec(memory_space=pltpu.VMEM)
    return pl.pallas_call(
        functools.partial(kernel, dims),
        out_shape=(
            jax.ShapeDtypeStruct((TOK, cols), bf16),
            jax.ShapeDtypeStruct((TOK, ch), bf16),
            jax.ShapeDtypeStruct((TOK, ch), bf16),
            jax.ShapeDtypeStruct((TOK, ch), bf16),
            jax.ShapeDtypeStruct((TOK, ch), f32),
            jax.ShapeDtypeStruct((gwr, cols), f32),
        ),
        in_specs=[vmem] * 6,
        out_specs=[vmem] * 6,
        scratch_shapes=[
            pltpu.VMEM((2 * ch, TOK), bf16),
            pltpu.VMEM((2 * ch, TOK), bf16),
            pltpu.VMEM((2 * ch, TOK), f32),
            pltpu.VMEM((OWN, 2 * n, TOK), f32),
            pltpu.VMEM((OWN, 2 * n, TOK), f32),
            pltpu.VMEM((OWN, n, TOK, 2 * TOK), bf16),
            pltpu.VMEM((ch, TOK), f32),
            pltpu.VMEM((ch, TOK), f32),
            pltpu.VMEM((nt - 1, ch, TOK), bf16),
            pltpu.VMEM((nt - 1, ch, TOK), bf16),
            pltpu.VMEM((ch, TOK), f32),
            pltpu.VMEM((ch, TOK), f32),
            pltpu.VMEM((ch, TOK), f32),
            pltpu.VMEM((ch, TOK), f32),
            pltpu.VMEM((2 * ch, TOK), f32),
            pltpu.VMEM((2 * ch, TOK), bf16),
            pltpu.VMEM((2 * ch, TOK), bf16),
            pltpu.VMEM((every, TOK), bf16),
            pltpu.VMEM((group, TOK, cols), bf16),
            pltpu.VMEM((group, ny * nz * gwr, TOK), bf16),
            pltpu.VMEM((ny * nz * gwr, cols), f32),
            pltpu.VMEM((ny - 1, tall, cols), bf16),
            pltpu.VMEM((ny - 1, tall, cols), bf16),
            pltpu.VMEM((gwr, cols), bf16),
            pltpu.VMEM((gwr, cols), bf16),
            pltpu.SemaphoreType.DMA((8,)),
            pltpu.SemaphoreType.DMA((8,)),
            pltpu.SemaphoreType.DMA((nt - 1,)),
            pltpu.SemaphoreType.DMA((nt - 1,)),
            pltpu.SemaphoreType.DMA((nt - 1,)),
            pltpu.SemaphoreType.DMA((nt - 1,)),
        ],
        compiler_params=pltpu.CompilerParams(
            collective_id=0, has_side_effects=True, vmem_limit_bytes=56 * 1024 * 1024
        ),
    )(q, k, v, f, w, go)


def solution(mesh, dims=(4, 4, 2, 2, 4)):
    return jax.shard_map(
        functools.partial(per_device, dims),
        mesh=mesh,
        in_specs=(
            P("ctx", "tp"),
            P("ctx", "tp"),
            P("ctx", "tp"),
            P("ctx", "tp"),
            P(None, "tp"),
            P("ctx", "tp"),
        ),
        out_specs=(P("ctx", "tp"),) * 6,
        check_vma=False,
    )
```

```python
import functools

import jax
import jax.numpy as jnp
from jax import lax
from jax.experimental import pallas as pl
from jax.experimental.pallas import tpu as pltpu
from jax.sharding import PartitionSpec as P

f32 = jnp.float32
bf16 = jnp.bfloat16
MESH = pl.DeviceIdType.MESH
OWN = 8
TOK = 128


def dot_nn(a, b):
    return lax.dot_general(a, b, (((1,), (0,)), ((), ())), preferred_element_type=f32)


def dot_nt(a, b):
    return lax.dot_general(a, b, (((1,), (1,)), ((), ())), preferred_element_type=f32)


def kernel(
    dims,
    q_ref,
    k_ref,
    v_ref,
    f_ref,
    wh_ref,
    go_ref,
    out_ref,
    gq_ref,
    gk_ref,
    gv_ref,
    gf_ref,
    gw_ref,
    s1_ref,
    r1_ref,
    xf_ref,
    xpad_ref,
    gpad_ref,
    t_ref,
    qt_ref,
    gm_ref,
    ps_ref,
    pr_ref,
    gs_ref,
    gr_ref,
    ys_ref,
    yr_ref,
    pqf_ref,
    pqs_ref,
    pqr_ref,
    mix_ref,
    ml_ref,
    w_ref,
    b_ref,
    a_ref,
    cf_ref,
    cs_ref,
    cr_ref,
    zs_ref,
    zr_ref,
    send_sem,
    recv_sem,
    tp_send,
    tp_recv,
    mx_send,
    mx_recv,
    a_send,
    a_recv,
    c_send,
    c_recv,
    z_send,
    z_recv,
    local_sem,
):
    nx, ny, nz, nc, nt = dims
    n = nx * ny * nz * nc
    ch = OWN * n
    cols = go_ref.shape[1]
    gwr = gw_ref.shape[0]
    group = nx * nc
    me = lax.axis_index("ctx")
    tp = lax.axis_index("tp")
    core = me % nc
    zh = me // nc % nz
    yy = me // (nc * nz) % ny
    xx = me // (nc * nz * ny)
    slot = xx * nc + core

    row_id = lax.broadcasted_iota(jnp.int32, (TOK, TOK), 0)
    col_id = lax.broadcasted_iota(jnp.int32, (TOK, TOK), 1)
    eye = (row_id == col_id).astype(f32).astype(bf16)
    rev = (row_id + col_id == TOK - 1).astype(f32).astype(bf16)
    lower = col_id >= row_id

    def remote(src, dst, ssem, rsem, device):
        return pltpu.make_async_remote_copy(
            src_ref=src,
            dst_ref=dst,
            send_sem=ssem,
            recv_sem=rsem,
            device_id=device,
            device_id_type=MESH,
        )

    def wait_rows(ref, rows, sem):
        pltpu.make_async_copy(ref.at[pl.ds(0, rows)], ref.at[pl.ds(0, rows)], sem).wait()

    def spread(src, dst, size, src_block, dst_block, index):
        def one(step, carry):
            peer = (me + step) % n
            remote(
                src.at[pl.ds(pl.multiple_of(src_block(peer) * size, size), size)],
                dst.at[pl.ds(pl.multiple_of(dst_block * size, size), size)],
                send_sem.at[index],
                recv_sem.at[index],
                {"ctx": peer},
            ).start()
            return carry

        lax.fori_loop(1, n, one, 0)

    def member(step):
        other = (slot + step) % group
        return ((other // nc * ny + yy) * nz + zh) * nc + other % nc

    barrier = pltpu.get_barrier_semaphore()

    def greet(step, carry):
        pl.semaphore_signal(
            barrier, inc=1, device_id={"ctx": (me + step) % n}, device_id_type=MESH
        )
        return carry

    lax.fori_loop(1, n, greet, 0)
    for step in range(1, nt):
        pl.semaphore_signal(
            barrier, inc=1, device_id={"tp": (tp + step) % nt}, device_id_type=MESH
        )

    weight_copy = pltpu.make_async_copy(wh_ref, w_ref, local_sem)
    weight_copy.start()

    for j in range(ch // TOK):
        lanes = pl.ds(j * TOK, TOK)
        gated = (k_ref[:, lanes].astype(f32) * v_ref[:, lanes].astype(f32)).astype(bf16)
        gated_t = dot_nt(eye, gated).reshape(TOK // OWN, OWN, TOK)
        filter_t = dot_nt(eye, f_ref[:, lanes].astype(bf16)).reshape(TOK // OWN, OWN, TOK)
        both = jnp.concatenate([gated_t, filter_t], axis=1)
        s1_ref[pl.ds(2 * j * TOK, 2 * TOK), :] = both.reshape(2 * TOK, TOK).astype(bf16)
        qt_ref[pl.ds(j * TOK, TOK), :] = dot_nt(eye, q_ref[:, lanes])

    pl.semaphore_wait(barrier, n - 1 + nt - 1)
    spread(s1_ref, r1_ref, 2 * OWN, lambda peer: peer, me, 0)

    part = min(ch, 512)
    weight_copy.wait()

    def partial(target, write):
        def rows(i, carry):
            start = pl.multiple_of(target * ch + i * part, part)
            write(
                pl.ds(pl.multiple_of(i * part, part), part),
                dot_nt(w_ref[pl.ds(start, part), :], go_ref[...]),
            )
            return carry

        lax.fori_loop(0, ch // part, rows, 0)

    for step in range(1, nt):
        peer = (tp + step) % nt

        def put(rows, value, step=step):
            ps_ref[step - 1, rows, :] = value.astype(bf16)

        partial(peer, put)
        remote(
            ps_ref.at[step - 1],
            pr_ref.at[step - 1],
            tp_send.at[step - 1],
            tp_recv.at[step - 1],
            {"tp": peer},
        ).start()

    def put_own(rows, value):
        gm_ref[rows, :] = value

    partial(tp, put_own)

    def share(step, carry):
        remote(
            go_ref, b_ref.at[slot], send_sem.at[4], recv_sem.at[4], {"ctx": member(step)}
        ).start()
        return carry

    lax.fori_loop(1, group, share, 0)

    wait_rows(r1_ref, (n - 1) * 2 * OWN, recv_sem.at[0])
    mine = pl.ds(pl.multiple_of(me * 2 * OWN, 2 * OWN), 2 * OWN)
    mine8 = pl.ds(pl.multiple_of(me * OWN, OWN), OWN)
    r1_ref[mine, :] = s1_ref[mine, :]
    xf_ref[...] = r1_ref[...].astype(f32)

    def toeplitz(c, first, lanes):
        def block(d, before):
            line = xf_ref[pl.ds(d * 2 * OWN + first + c, 1), :]
            now = pltpu.roll(
                jnp.broadcast_to(line, (TOK, TOK)), 0, 1, stride=1, stride_axis=0
            )
            t_ref[c, d, :, lanes] = jnp.where(lower, now, before).astype(bf16)
            return now

        lax.fori_loop(0, n, block, jnp.zeros((TOK, TOK), f32), unroll=n)

    def convolve(pad, c, lanes, width):
        left = jnp.concatenate(
            [pad[c, pl.ds(n - i, n), :].astype(bf16) for i in range(n)], axis=1
        )
        return dot_nn(left, t_ref[c, :, :, lanes].reshape(n * TOK, width))

    def forward(c, carry):
        xpad_ref[c, pl.ds(0, n), :] = jnp.zeros((n, TOK), f32)
        xpad_ref[c, pl.ds(n, n), :] = xf_ref[pl.ds(c, n, stride=2 * OWN), :]
        toeplitz(c, OWN, pl.ds(0, TOK))
        ys_ref[pl.ds(c, n, stride=OWN), :] = convolve(xpad_ref, c, pl.ds(0, TOK), TOK)
        return carry

    lax.fori_loop(0, OWN, forward, 0)
    spread(ys_ref, yr_ref, OWN, lambda peer: peer, me, 2)

    for step in range(1, nt):
        remote(
            ps_ref.at[step - 1],
            pr_ref.at[step - 1],
            tp_send.at[step - 1],
            tp_recv.at[step - 1],
            {"tp": (tp + step) % nt},
        ).wait_recv()

    def sum_rows(i, carry):
        rows = pl.ds(pl.multiple_of(i * TOK, TOK), TOK)
        total = gm_ref[rows, :]
        for step in range(1, nt):
            total = total + pr_ref[step - 1, rows, :].astype(f32)
        gm_ref[rows, :] = total
        gs_ref[rows, :] = dot_nn((total * qt_ref[rows, :]).astype(bf16), rev)
        return carry

    lax.fori_loop(0, ch // TOK, sum_rows, 0)
    spread(gs_ref, gr_ref, OWN, lambda peer: peer, n - 1 - me, 1)

    wait_rows(yr_ref, (n - 1) * OWN, recv_sem.at[2])
    yr_ref[mine8, :] = ys_ref[mine8, :]
    blocks = ny * nz
    per = TOK // (nc * gwr)

    def mix(i, carry):
        rows = pl.ds(pl.multiple_of(i * TOK, TOK), TOK)
        mixed = (qt_ref[rows, :] * yr_ref[rows, :]).astype(bf16)
        mix_ref[tp, pl.ds(i * per, per)] = mixed.reshape(per, nc, gwr, TOK)
        return carry

    lax.fori_loop(0, ch // TOK, mix, 0)

    for step in range(1, nt):
        remote(
            mix_ref.at[tp],
            mix_ref.at[tp],
            mx_send.at[step - 1],
            mx_recv.at[step - 1],
            {"tp": (tp + step) % nt},
        ).start()

    def feed(source):
        for core_step in range(nc):
            to_core = (core + core_step) % nc
            copy = remote(
                mix_ref.at[source, :, to_core],
                a_ref.at[slot],
                a_send,
                a_recv,
                {"ctx": ((source * ny + yy) * nz + zh) * nc + to_core},
            )
            if core_step == 0:

                @pl.when(xx != source)
                def _(copy=copy):
                    copy.start()

            else:
                copy.start()

    def other_blocks(c, carry):
        toeplitz(c, 0, pl.ds(TOK, TOK))
        return carry

    feed(tp)
    done = 0
    for step in range(1, nt):
        until = OWN * step // (nt - 1)
        lax.fori_loop(done, until, other_blocks, 0)
        done = until
        source = (tp + nt - step) % nt
        remote(
            mix_ref.at[source],
            mix_ref.at[source],
            mx_send.at[step - 1],
            mx_recv.at[step - 1],
            {"tp": (tp + step) % nt},
        ).wait_recv()
        feed(source)

    wait_rows(gr_ref, (n - 1) * OWN, recv_sem.at[1])
    gr_ref[pl.ds(pl.multiple_of((n - 1 - me) * OWN, OWN), OWN), :] = gs_ref[mine8, :]

    def backward(c, carry):
        gpad_ref[c, pl.ds(0, n), :] = jnp.zeros((n, TOK), f32)
        gpad_ref[c, pl.ds(n, n), :] = gr_ref[pl.ds(c, n, stride=OWN), :]
        acc = convolve(gpad_ref, c, pl.ds(0, 2 * TOK), 2 * TOK)
        pqf_ref[pl.ds(c, n, stride=2 * OWN), :] = acc[:, :TOK]
        pqf_ref[pl.ds(OWN + c, n, stride=2 * OWN), :] = acc[:, TOK:]
        return carry

    lax.fori_loop(0, OWN, backward, 0)
    pqs_ref[...] = pqf_ref[...].astype(bf16)

    wait_rows(b_ref, group - 1, recv_sem.at[4])
    wait_rows(a_ref, group - 1, a_recv)
    b_ref[slot] = go_ref[...]
    a_ref[slot] = mix_ref[xx, :, core]

    wide = min(cols, 256)
    tiles = cols // wide
    tall = nz * gwr

    def send_tile(i, y_step):
        other = (yy + y_step) % ny
        return remote(
            cs_ref.at[i, y_step - 1],
            cr_ref.at[i, y_step - 1],
            c_send.at[i],
            c_recv.at[i],
            {"ctx": ((xx * ny + other) * nz + zh) * nc + core},
        )

    def weight(i, carry):
        columns = pl.ds(pl.multiple_of(i * wide, wide), wide)
        acc = jnp.zeros((blocks * gwr, wide), f32)
        for source in range(group):
            left = a_ref[source].reshape(blocks * gwr, TOK)
            acc = acc + dot_nn(left, b_ref[source, :, columns])
        cf_ref[i] = acc
        for y_step in range(1, ny):
            other = (yy + y_step) % ny
            rows = pl.ds(pl.multiple_of(other * tall, tall), tall)
            cs_ref[i, y_step - 1] = cf_ref[i, rows, :].astype(bf16)
            send_tile(i, y_step).start()
        return carry

    lax.fori_loop(0, tiles, weight, 0)

    spread(pqs_ref, pqr_ref, 2 * OWN, lambda peer: n - 1 - peer, me, 3)

    far = (zh + 1) % nz

    def across(i):
        return remote(
            zs_ref.at[i],
            zr_ref.at[i],
            z_send.at[i],
            z_recv.at[i],
            {"ctx": ((xx * ny + yy) * nz + far) * nc + core},
        )

    def over_y(i, carry):
        pltpu.make_async_copy(cr_ref.at[i], cr_ref.at[i], c_recv.at[i]).wait()

        def total(level):
            rows = pl.ds(pl.multiple_of(level * gwr, gwr), gwr)
            value = cf_ref[i, pl.ds(pl.multiple_of(yy * tall + level * gwr, gwr), gwr), :]
            for y_step in range(1, ny):
                value = value + cr_ref[i, y_step - 1, rows, :].astype(f32)
            return value

        zs_ref[i] = total(far).astype(bf16)
        across(i).start()
        gw_ref[:, pl.ds(pl.multiple_of(i * wide, wide), wide)] = total(zh)
        return carry

    lax.fori_loop(0, tiles, over_y, 0)

    def turn(source, carry):
        left = dot_nt(eye, mix_ref[source].reshape(ch, TOK)).astype(bf16)
        ml_ref[:, pl.ds(pl.multiple_of(source * ch, ch), ch)] = left
        return carry

    lax.fori_loop(0, nt, turn, 0)

    def project(i, carry):
        columns = pl.ds(pl.multiple_of(i * wide, wide), wide)
        out_ref[:, columns] = dot_nn(ml_ref[...], w_ref[:, columns]).astype(bf16)
        return carry

    lax.fori_loop(0, tiles, project, 0)

    def query(j, carry):
        rows = pl.ds(pl.multiple_of(j * TOK, TOK), TOK)
        grad = (gm_ref[rows, :] * yr_ref[rows, :]).astype(bf16)
        gq_ref[:, rows] = dot_nt(eye, grad).astype(bf16)
        return carry

    lax.fori_loop(0, ch // TOK, query, 0)
    wait_rows(pqr_ref, (n - 1) * 2 * OWN, recv_sem.at[3])
    back = pl.ds(pl.multiple_of((n - 1 - me) * 2 * OWN, 2 * OWN), 2 * OWN)
    pqr_ref[mine, :] = pqs_ref[back, :]

    def finish(j, carry):
        lanes = pl.ds(pl.multiple_of(j * TOK, TOK), TOK)
        both = pqr_ref[pl.ds(pl.multiple_of(2 * j * TOK, TOK), 2 * TOK), :].astype(f32)
        both = both.reshape(TOK // OWN, 2 * OWN, TOK)
        grad_gated = dot_nt(rev, both[:, :OWN].reshape(TOK, TOK).astype(bf16))
        gf_ref[:, lanes] = dot_nt(rev, both[:, OWN:].reshape(TOK, TOK).astype(bf16))
        gk_ref[:, lanes] = (grad_gated * v_ref[:, lanes].astype(f32)).astype(bf16)
        gv_ref[:, lanes] = (grad_gated * k_ref[:, lanes].astype(f32)).astype(bf16)
        return carry

    lax.fori_loop(0, ch // TOK, finish, 0)

    def over_z(i, carry):
        across(i).wait_recv()
        columns = pl.ds(pl.multiple_of(i * wide, wide), wide)
        gw_ref[:, columns] = gw_ref[:, columns] + zr_ref[i].astype(f32)
        return carry

    lax.fori_loop(0, tiles, over_z, 0)

    wait_rows(s1_ref, (n - 1) * 2 * OWN, send_sem.at[0])
    wait_rows(gs_ref, (n - 1) * OWN, send_sem.at[1])
    wait_rows(ys_ref, (n - 1) * OWN, send_sem.at[2])
    wait_rows(pqs_ref, (n - 1) * 2 * OWN, send_sem.at[3])
    wait_rows(b_ref, group - 1, send_sem.at[4])

    wait_rows(a_ref, group - 1, a_send)

    def left_tile(i, carry):
        pltpu.make_async_copy(cs_ref.at[i], cs_ref.at[i], c_send.at[i]).wait()
        across(i).wait_send()
        return carry

    lax.fori_loop(0, tiles, left_tile, 0)
    for step in range(1, nt):
        peer = {"tp": (tp + step) % nt}
        remote(
            ps_ref.at[step - 1],
            pr_ref.at[step - 1],
            tp_send.at[step - 1],
            tp_recv.at[step - 1],
            peer,
        ).wait_send()
        remote(
            mix_ref.at[tp],
            mix_ref.at[tp],
            mx_send.at[step - 1],
            mx_recv.at[step - 1],
            peer,
        ).wait_send()


def place_kernel(*refs):
    copies = [
        pltpu.make_async_copy(refs[i], refs[6 + i], refs[12].at[i]) for i in range(6)
    ]
    for copy in copies:
        copy.start()
    for copy in copies:
        copy.wait()


def place(arrays):
    anywhere = pl.BlockSpec(memory_space=pl.ANY)
    return pl.pallas_call(
        place_kernel,
        out_shape=tuple(jax.ShapeDtypeStruct(a.shape, a.dtype) for a in arrays),
        in_specs=[anywhere] * 6,
        out_specs=[pl.BlockSpec(memory_space=pltpu.VMEM)] * 6,
        scratch_shapes=[pltpu.SemaphoreType.DMA((6,))],
        compiler_params=pltpu.CompilerParams(vmem_limit_bytes=60 * 1024 * 1024),
    )(*arrays)


def per_device(dims, q, k, v, f, w, go):
    nx, ny, nz, nc, nt = dims
    n = nx * ny * nz * nc
    ch = OWN * n
    every = ch * nt
    cols = go.shape[1]
    gwr = every // n
    group = nx * nc
    tall = nz * gwr
    wide = min(cols, 256)
    tiles = cols // wide
    vmem = pl.BlockSpec(memory_space=pltpu.VMEM)
    results = pl.pallas_call(
        functools.partial(kernel, dims),
        out_shape=(
            jax.ShapeDtypeStruct((TOK, cols), bf16),
            jax.ShapeDtypeStruct((TOK, ch), bf16),
            jax.ShapeDtypeStruct((TOK, ch), bf16),
            jax.ShapeDtypeStruct((TOK, ch), bf16),
            jax.ShapeDtypeStruct((TOK, ch), f32),
            jax.ShapeDtypeStruct((gwr, cols), f32),
        ),
        in_specs=[vmem] * 4 + [pl.BlockSpec(memory_space=pl.ANY), vmem],
        out_specs=[vmem] * 6,
        scratch_shapes=[
            pltpu.VMEM((2 * ch, TOK), bf16),
            pltpu.VMEM((2 * ch, TOK), bf16),
            pltpu.VMEM((2 * ch, TOK), f32),
            pltpu.VMEM((OWN, 2 * n, TOK), f32),
            pltpu.VMEM((OWN, 2 * n, TOK), f32),
            pltpu.VMEM((OWN, n, TOK, 2 * TOK), bf16),
            pltpu.VMEM((ch, TOK), f32),
            pltpu.VMEM((ch, TOK), f32),
            pltpu.VMEM((nt - 1, ch, TOK), bf16),
            pltpu.VMEM((nt - 1, ch, TOK), bf16),
            pltpu.VMEM((ch, TOK), f32),
            pltpu.VMEM((ch, TOK), f32),
            pltpu.VMEM((ch, TOK), f32),
            pltpu.VMEM((ch, TOK), f32),
            pltpu.VMEM((2 * ch, TOK), f32),
            pltpu.VMEM((2 * ch, TOK), bf16),
            pltpu.VMEM((2 * ch, TOK), bf16),
            pltpu.VMEM((nt, ny * nz, nc, gwr, TOK), bf16),
            pltpu.VMEM((TOK, every), bf16),
            pltpu.VMEM((every, cols), bf16),
            pltpu.VMEM((group, TOK, cols), bf16),
            pltpu.VMEM((group, ny * nz, gwr, TOK), bf16),
            pltpu.VMEM((tiles, ny * nz * gwr, wide), f32),
            pltpu.VMEM((tiles, ny - 1, tall, wide), bf16),
            pltpu.VMEM((tiles, ny - 1, tall, wide), bf16),
            pltpu.VMEM((tiles, gwr, wide), bf16),
            pltpu.VMEM((tiles, gwr, wide), bf16),
            pltpu.SemaphoreType.DMA((5,)),
            pltpu.SemaphoreType.DMA((5,)),
            pltpu.SemaphoreType.DMA((nt - 1,)),
            pltpu.SemaphoreType.DMA((nt - 1,)),
            pltpu.SemaphoreType.DMA((nt - 1,)),
            pltpu.SemaphoreType.DMA((nt - 1,)),
            pltpu.SemaphoreType.DMA,
            pltpu.SemaphoreType.DMA,
            pltpu.SemaphoreType.DMA((tiles,)),
            pltpu.SemaphoreType.DMA((tiles,)),
            pltpu.SemaphoreType.DMA((tiles,)),
            pltpu.SemaphoreType.DMA((tiles,)),
            pltpu.SemaphoreType.DMA,
        ],
        compiler_params=pltpu.CompilerParams(
            collective_id=0, has_side_effects=True, vmem_limit_bytes=56 * 1024 * 1024
        ),
    )(q, k, v, f, w, go)
    return place(results)


def solution(mesh, dims=(4, 4, 2, 2, 4)):
    return jax.shard_map(
        functools.partial(per_device, dims),
        mesh=mesh,
        in_specs=(
            P("ctx", "tp"),
            P("ctx", "tp"),
            P("ctx", "tp"),
            P("ctx", "tp"),
            P(None, "tp"),
            P("ctx", "tp"),
        ),
        out_specs=(P("ctx", "tp"),) * 6,
        check_vma=False,
    )
```

```python
import functools

import jax
import jax.numpy as jnp
from jax import lax
from jax.experimental import pallas as pl
from jax.experimental.pallas import tpu as pltpu
from jax.sharding import PartitionSpec as P

f32 = jnp.float32
bf16 = jnp.bfloat16
MESH = pl.DeviceIdType.MESH
OWN = 8
TOK = 128


def dot_nn(a, b):
    return lax.dot_general(a, b, (((1,), (0,)), ((), ())), preferred_element_type=f32)


def dot_nt(a, b):
    return lax.dot_general(a, b, (((1,), (1,)), ((), ())), preferred_element_type=f32)


def kernel(
    dims,
    q_ref,
    k_ref,
    v_ref,
    f_ref,
    wh_ref,
    go_ref,
    out_ref,
    gq_ref,
    gk_ref,
    gv_ref,
    gf_ref,
    gw_ref,
    s1_ref,
    r1_ref,
    xf_ref,
    xpad_ref,
    gpad_ref,
    t_ref,
    qt_ref,
    gm_ref,
    ps_ref,
    pr_ref,
    gsb_ref,
    grb_ref,
    gr_ref,
    ys_ref,
    ysb_ref,
    yrb_ref,
    yr_ref,
    pqf_ref,
    pqs_ref,
    pqr_ref,
    mix_ref,
    ml_ref,
    w_ref,
    b_ref,
    a_ref,
    cf_ref,
    cs_ref,
    cr_ref,
    zs_ref,
    zr_ref,
    send_sem,
    recv_sem,
    tp_send,
    tp_recv,
    mx_send,
    mx_recv,
    b_send,
    b_recv,
    a_send,
    a_recv,
    c_send,
    c_recv,
    z_send,
    z_recv,
    local_sem,
):
    nx, ny, nz, nc, nt = dims
    n = nx * ny * nz * nc
    ch = OWN * n
    cols = go_ref.shape[1]
    gwr = gw_ref.shape[0]
    group = nx * nc
    me = lax.axis_index("ctx")
    tp = lax.axis_index("tp")
    core = me % nc
    zh = me // nc % nz
    yy = me // (nc * nz) % ny
    xx = me // (nc * nz * ny)
    slot = xx * nc + core

    row_id = lax.broadcasted_iota(jnp.int32, (TOK, TOK), 0)
    col_id = lax.broadcasted_iota(jnp.int32, (TOK, TOK), 1)
    eye = (row_id == col_id).astype(f32).astype(bf16)
    rev = (row_id + col_id == TOK - 1).astype(f32).astype(bf16)
    lower = col_id >= row_id

    def remote(src, dst, ssem, rsem, device):
        return pltpu.make_async_remote_copy(
            src_ref=src,
            dst_ref=dst,
            send_sem=ssem,
            recv_sem=rsem,
            device_id=device,
            device_id_type=MESH,
        )

    def wait_rows(ref, rows, sem):
        pltpu.make_async_copy(ref.at[pl.ds(0, rows)], ref.at[pl.ds(0, rows)], sem).wait()

    def spread8(src, dst, dst_block, index):
        def one(step, carry):
            peer = (me + step) % n
            remote(
                src.at[peer],
                dst.at[dst_block],
                send_sem.at[index],
                recv_sem.at[index],
                {"ctx": peer},
            ).start()
            return carry

        lax.fori_loop(1, n, one, 0)

    def spread(src, dst, size, src_block, dst_block, index):
        def one(step, carry):
            peer = (me + step) % n
            remote(
                src.at[pl.ds(pl.multiple_of(src_block(peer) * size, size), size)],
                dst.at[pl.ds(pl.multiple_of(dst_block * size, size), size)],
                send_sem.at[index],
                recv_sem.at[index],
                {"ctx": peer},
            ).start()
            return carry

        lax.fori_loop(1, n, one, 0)

    def member(step):
        other = (slot + step) % group
        return ((other // nc * ny + yy) * nz + zh) * nc + other % nc

    barrier = pltpu.get_barrier_semaphore()

    def greet(step, carry):
        pl.semaphore_signal(
            barrier, inc=1, device_id={"ctx": (me + step) % n}, device_id_type=MESH
        )
        return carry

    lax.fori_loop(1, n, greet, 0)
    for step in range(1, nt):
        pl.semaphore_signal(
            barrier, inc=1, device_id={"tp": (tp + step) % nt}, device_id_type=MESH
        )

    weight_copy = pltpu.make_async_copy(wh_ref, w_ref, local_sem)
    weight_copy.start()

    for j in range(ch // TOK):
        lanes = pl.ds(j * TOK, TOK)
        gated = (k_ref[:, lanes].astype(f32) * v_ref[:, lanes].astype(f32)).astype(bf16)
        gated_t = dot_nt(eye, gated).reshape(TOK // OWN, OWN, TOK)
        filter_t = dot_nt(eye, f_ref[:, lanes].astype(bf16)).reshape(TOK // OWN, OWN, TOK)
        both = jnp.concatenate([gated_t, filter_t], axis=1)
        s1_ref[pl.ds(2 * j * TOK, 2 * TOK), :] = both.reshape(2 * TOK, TOK).astype(bf16)
        qt_ref[pl.ds(j * TOK, TOK), :] = dot_nt(eye, q_ref[:, lanes])

    pl.semaphore_wait(barrier, n - 1 + nt - 1)
    spread(s1_ref, r1_ref, 2 * OWN, lambda peer: peer, me, 0)

    part = min(ch, 512)
    weight_copy.wait()

    def partial(target, write):
        def rows(i, carry):
            start = pl.multiple_of(target * ch + i * part, part)
            write(
                pl.ds(pl.multiple_of(i * part, part), part),
                dot_nt(w_ref[pl.ds(start, part), :], go_ref[...]),
            )
            return carry

        lax.fori_loop(0, ch // part, rows, 0)

    for step in range(1, nt):

        def put(rows, value, step=step):
            ps_ref[step - 1, rows, :] = value.astype(bf16)

        partial((tp + step) % nt, put)

    def put_own(rows, value):
        gm_ref[rows, :] = value

    partial(tp, put_own)

    wait_rows(r1_ref, (n - 1) * 2 * OWN, recv_sem.at[0])
    mine = pl.ds(pl.multiple_of(me * 2 * OWN, 2 * OWN), 2 * OWN)
    for step in range(1, nt):
        remote(
            ps_ref.at[step - 1],
            pr_ref.at[step - 1],
            tp_send.at[step - 1],
            tp_recv.at[step - 1],
            {"tp": (tp + step) % nt},
        ).start()

    def along(step):
        return remote(
            go_ref,
            b_ref.at[slot],
            b_send,
            b_recv,
            {"ctx": (((xx + step) % nx * ny + yy) * nz + zh) * nc + core},
        )

    for step in range(1, nx):
        along(step).start()
    r1_ref[mine, :] = s1_ref[mine, :]
    xf_ref[...] = r1_ref[...].astype(f32)

    def toeplitz(c, first, lanes):
        def block(d, before):
            line = xf_ref[pl.ds(d * 2 * OWN + first + c, 1), :]
            now = pltpu.roll(
                jnp.broadcast_to(line, (TOK, TOK)), 0, 1, stride=1, stride_axis=0
            )
            t_ref[c, d, :, lanes] = jnp.where(lower, now, before).astype(bf16)
            return now

        lax.fori_loop(0, n, block, jnp.zeros((TOK, TOK), f32), unroll=n)

    def convolve(pad, c, lanes, width):
        left = jnp.concatenate(
            [pad[c, pl.ds(n - i, n), :].astype(bf16) for i in range(n)], axis=1
        )
        return dot_nn(left, t_ref[c, :, :, lanes].reshape(n * TOK, width))

    def forward(c, carry):
        xpad_ref[c, pl.ds(0, n), :] = jnp.zeros((n, TOK), f32)
        xpad_ref[c, pl.ds(n, n), :] = xf_ref[pl.ds(c, n, stride=2 * OWN), :]
        toeplitz(c, OWN, pl.ds(0, TOK))
        ys_ref[pl.ds(c, n, stride=OWN), :] = convolve(xpad_ref, c, pl.ds(0, TOK), TOK)
        return carry

    lax.fori_loop(0, OWN, forward, 0)
    ysb_ref[...] = ys_ref[...].reshape(n, OWN, TOK).astype(bf16)
    spread8(ysb_ref, yrb_ref, me, 2)

    for step in range(1, nt):
        remote(
            ps_ref.at[step - 1],
            pr_ref.at[step - 1],
            tp_send.at[step - 1],
            tp_recv.at[step - 1],
            {"tp": (tp + step) % nt},
        ).wait_recv()

    def sum_rows(i, carry):
        rows = pl.ds(pl.multiple_of(i * TOK, TOK), TOK)
        total = gm_ref[rows, :]
        for step in range(1, nt):
            total = total + pr_ref[step - 1, rows, :].astype(f32)
        gm_ref[rows, :] = total
        back = dot_nn((total * qt_ref[rows, :]).astype(bf16), rev)
        gsb_ref[pl.ds(i * (TOK // OWN), TOK // OWN)] = back.reshape(
            TOK // OWN, OWN, TOK
        ).astype(bf16)
        return carry

    lax.fori_loop(0, ch // TOK, sum_rows, 0)
    spread8(gsb_ref, grb_ref, n - 1 - me, 1)

    wait_rows(b_ref, nx - 1, b_recv)
    b_ref[slot] = go_ref[...]

    def to_core(step, x_step):
        block = b_ref.at[(xx + x_step) % nx * nc + core]
        return remote(
            block,
            block,
            send_sem.at[4],
            recv_sem.at[4],
            {"ctx": me - core + (core + step) % nc},
        )

    for step in range(1, nc):
        for x_step in range(nx):
            to_core(step, x_step).start()

    wait_rows(yrb_ref, n - 1, recv_sem.at[2])
    yrb_ref[me] = ysb_ref[me]
    yr_ref[...] = yrb_ref[...].astype(f32).reshape(ch, TOK)
    blocks = ny * nz
    per = TOK // (nc * gwr)

    def mix(i, carry):
        rows = pl.ds(pl.multiple_of(i * TOK, TOK), TOK)
        mixed = (qt_ref[rows, :] * yr_ref[rows, :]).astype(bf16)
        mix_ref[tp, pl.ds(i * per, per)] = mixed.reshape(per, nc, gwr, TOK)
        return carry

    lax.fori_loop(0, ch // TOK, mix, 0)

    half = blocks // 2

    def pass_on(source, way, hop, piece):
        rows = mix_ref.at[source, pl.ds(piece * half, half)]
        return remote(
            rows,
            rows,
            mx_send.at[way, hop, piece],
            mx_recv.at[way, hop, piece],
            {"tp": jnp.clip(tp + (1 - 2 * way), 0, nt - 1)},
        )

    def has_next(way):
        return tp < nt - 1 if way == 0 else tp > 0

    def has_hop(way, hop):
        return tp >= hop if way == 0 else tp + hop < nt

    for piece in range(2):
        for way in range(2):

            @pl.when(has_next(way))
            def _(way=way, piece=piece):
                pass_on(tp, way, 0, piece).start()

    def feed(source, piece):
        part_rows = pl.ds(piece * half, half)
        for core_step in range(nc):
            to_core = (core + core_step) % nc
            copy = remote(
                mix_ref.at[source, part_rows, to_core],
                a_ref.at[slot, part_rows],
                a_send,
                a_recv,
                {"ctx": ((source * ny + yy) * nz + zh) * nc + to_core},
            )
            if core_step == 0:

                @pl.when(xx != source)
                def _(copy=copy):
                    copy.start()

            else:
                copy.start()

    def other_blocks(c, carry):
        toeplitz(c, 0, pl.ds(TOK, TOK))
        return carry

    feed(tp, 0)
    feed(tp, 1)
    done = 0
    for hop in range(1, nt):
        until = OWN * hop // (nt - 1)
        lax.fori_loop(done, until, other_blocks, 0)
        done = until
        for piece in range(2):
            for way in range(2):

                @pl.when(has_hop(way, hop))
                def _(way=way, hop=hop, piece=piece):
                    source = tp - hop * (1 - 2 * way)
                    pass_on(source, way, hop - 1, piece).wait_recv()
                    if hop < nt - 1:

                        @pl.when(has_next(way))
                        def _():
                            pass_on(source, way, hop, piece).start()

                    feed(source, piece)

    wait_rows(grb_ref, n - 1, recv_sem.at[1])
    grb_ref[n - 1 - me] = gsb_ref[me]
    gr_ref[...] = grb_ref[...].astype(f32).reshape(ch, TOK)

    def backward(c, carry):
        gpad_ref[c, pl.ds(0, n), :] = jnp.zeros((n, TOK), f32)
        gpad_ref[c, pl.ds(n, n), :] = gr_ref[pl.ds(c, n, stride=OWN), :]
        acc = convolve(gpad_ref, c, pl.ds(0, 2 * TOK), 2 * TOK)
        pqf_ref[pl.ds(c, n, stride=2 * OWN), :] = acc[:, :TOK]
        pqf_ref[pl.ds(OWN + c, n, stride=2 * OWN), :] = acc[:, TOK:]
        return carry

    lax.fori_loop(0, OWN, backward, 0)
    pqs_ref[...] = pqf_ref[...].astype(bf16)

    if nc > 1:
        wait_rows(b_ref, nx * (nc - 1), recv_sem.at[4])
    wait_rows(a_ref, group - 1, a_recv)
    a_ref[slot] = mix_ref[xx, :, core]

    wide = min(cols, 256)
    tiles = cols // wide
    tall = nz * gwr

    def send_tile(i, y_step):
        other = (yy + y_step) % ny
        return remote(
            cs_ref.at[i, y_step - 1],
            cr_ref.at[i, y_step - 1],
            c_send.at[i],
            c_recv.at[i],
            {"ctx": ((xx * ny + other) * nz + zh) * nc + core},
        )

    def weight(i, carry):
        columns = pl.ds(pl.multiple_of(i * wide, wide), wide)
        acc = jnp.zeros((blocks * gwr, wide), f32)
        for source in range(group):
            left = a_ref[source].reshape(blocks * gwr, TOK)
            acc = acc + dot_nn(left, b_ref[source, :, columns])
        cf_ref[i] = acc
        for y_step in range(1, ny):
            other = (yy + y_step) % ny
            rows = pl.ds(pl.multiple_of(other * tall, tall), tall)
            cs_ref[i, y_step - 1] = cf_ref[i, rows, :].astype(bf16)
            send_tile(i, y_step).start()
        return carry

    lax.fori_loop(0, tiles, weight, 0)

    spread(pqs_ref, pqr_ref, 2 * OWN, lambda peer: n - 1 - peer, me, 3)

    far = (zh + 1) % nz

    def across(i):
        return remote(
            zs_ref.at[i],
            zr_ref.at[i],
            z_send.at[i],
            z_recv.at[i],
            {"ctx": ((xx * ny + yy) * nz + far) * nc + core},
        )

    def over_y(i, carry):
        pltpu.make_async_copy(cr_ref.at[i], cr_ref.at[i], c_recv.at[i]).wait()

        def total(level):
            rows = pl.ds(pl.multiple_of(level * gwr, gwr), gwr)
            value = cf_ref[i, pl.ds(pl.multiple_of(yy * tall + level * gwr, gwr), gwr), :]
            for y_step in range(1, ny):
                value = value + cr_ref[i, y_step - 1, rows, :].astype(f32)
            return value

        zs_ref[i] = total(far).astype(bf16)
        across(i).start()
        gw_ref[:, pl.ds(pl.multiple_of(i * wide, wide), wide)] = total(zh)
        return carry

    lax.fori_loop(0, tiles, over_y, 0)

    def turn(source, carry):
        left = dot_nt(eye, mix_ref[source].reshape(ch, TOK)).astype(bf16)
        ml_ref[:, pl.ds(pl.multiple_of(source * ch, ch), ch)] = left
        return carry

    lax.fori_loop(0, nt, turn, 0)

    def project(i, carry):
        columns = pl.ds(pl.multiple_of(i * wide, wide), wide)
        out_ref[:, columns] = dot_nn(ml_ref[...], w_ref[:, columns]).astype(bf16)
        return carry

    lax.fori_loop(0, tiles, project, 0)

    def query(j, carry):
        rows = pl.ds(pl.multiple_of(j * TOK, TOK), TOK)
        grad = (gm_ref[rows, :] * yr_ref[rows, :]).astype(bf16)
        gq_ref[:, rows] = dot_nt(eye, grad).astype(bf16)
        return carry

    lax.fori_loop(0, ch // TOK, query, 0)
    wait_rows(pqr_ref, (n - 1) * 2 * OWN, recv_sem.at[3])
    back = pl.ds(pl.multiple_of((n - 1 - me) * 2 * OWN, 2 * OWN), 2 * OWN)
    pqr_ref[mine, :] = pqs_ref[back, :]

    def finish(j, carry):
        lanes = pl.ds(pl.multiple_of(j * TOK, TOK), TOK)
        both = pqr_ref[pl.ds(pl.multiple_of(2 * j * TOK, TOK), 2 * TOK), :].astype(f32)
        both = both.reshape(TOK // OWN, 2 * OWN, TOK)
        grad_gated = dot_nt(rev, both[:, :OWN].reshape(TOK, TOK).astype(bf16))
        gf_ref[:, lanes] = dot_nt(rev, both[:, OWN:].reshape(TOK, TOK).astype(bf16))
        gk_ref[:, lanes] = (grad_gated * v_ref[:, lanes].astype(f32)).astype(bf16)
        gv_ref[:, lanes] = (grad_gated * k_ref[:, lanes].astype(f32)).astype(bf16)
        return carry

    lax.fori_loop(0, ch // TOK, finish, 0)

    def over_z(i, carry):
        across(i).wait_recv()
        columns = pl.ds(pl.multiple_of(i * wide, wide), wide)
        gw_ref[:, columns] = gw_ref[:, columns] + zr_ref[i].astype(f32)
        return carry

    lax.fori_loop(0, tiles, over_z, 0)

    wait_rows(s1_ref, (n - 1) * 2 * OWN, send_sem.at[0])
    wait_rows(gsb_ref, n - 1, send_sem.at[1])
    wait_rows(ysb_ref, n - 1, send_sem.at[2])
    wait_rows(pqs_ref, (n - 1) * 2 * OWN, send_sem.at[3])
    wait_rows(b_ref, nx - 1, b_send)
    if nc > 1:
        wait_rows(b_ref, nx * (nc - 1), send_sem.at[4])

    wait_rows(a_ref, group - 1, a_send)

    def left_tile(i, carry):
        pltpu.make_async_copy(cs_ref.at[i], cs_ref.at[i], c_send.at[i]).wait()
        across(i).wait_send()
        return carry

    lax.fori_loop(0, tiles, left_tile, 0)
    for step in range(1, nt):
        peer = {"tp": (tp + step) % nt}
        remote(
            ps_ref.at[step - 1],
            pr_ref.at[step - 1],
            tp_send.at[step - 1],
            tp_recv.at[step - 1],
            peer,
        ).wait_send()
    for hop in range(nt - 1):
        for piece in range(2):
            for way in range(2):

                @pl.when(has_next(way) & has_hop(way, hop))
                def _(way=way, hop=hop, piece=piece):
                    pass_on(tp - hop * (1 - 2 * way), way, hop, piece).wait_send()


def place_kernel(*refs):
    copies = [
        pltpu.make_async_copy(refs[i], refs[6 + i], refs[12].at[i]) for i in range(6)
    ]
    for copy in copies:
        copy.start()
    for copy in copies:
        copy.wait()


def place(arrays):
    anywhere = pl.BlockSpec(memory_space=pl.ANY)
    return pl.pallas_call(
        place_kernel,
        out_shape=tuple(jax.ShapeDtypeStruct(a.shape, a.dtype) for a in arrays),
        in_specs=[anywhere] * 6,
        out_specs=[pl.BlockSpec(memory_space=pltpu.VMEM)] * 6,
        scratch_shapes=[pltpu.SemaphoreType.DMA((6,))],
        compiler_params=pltpu.CompilerParams(vmem_limit_bytes=60 * 1024 * 1024),
    )(*arrays)


def per_device(dims, q, k, v, f, w, go):
    nx, ny, nz, nc, nt = dims
    n = nx * ny * nz * nc
    ch = OWN * n
    every = ch * nt
    cols = go.shape[1]
    gwr = every // n
    group = nx * nc
    tall = nz * gwr
    wide = min(cols, 256)
    tiles = cols // wide
    vmem = pl.BlockSpec(memory_space=pltpu.VMEM)
    results = pl.pallas_call(
        functools.partial(kernel, dims),
        out_shape=(
            jax.ShapeDtypeStruct((TOK, cols), bf16),
            jax.ShapeDtypeStruct((TOK, ch), bf16),
            jax.ShapeDtypeStruct((TOK, ch), bf16),
            jax.ShapeDtypeStruct((TOK, ch), bf16),
            jax.ShapeDtypeStruct((TOK, ch), f32),
            jax.ShapeDtypeStruct((gwr, cols), f32),
        ),
        in_specs=[vmem] * 4 + [pl.BlockSpec(memory_space=pl.ANY), vmem],
        out_specs=[vmem] * 6,
        scratch_shapes=[
            pltpu.VMEM((2 * ch, TOK), bf16),
            pltpu.VMEM((2 * ch, TOK), bf16),
            pltpu.VMEM((2 * ch, TOK), f32),
            pltpu.VMEM((OWN, 2 * n, TOK), f32),
            pltpu.VMEM((OWN, 2 * n, TOK), f32),
            pltpu.VMEM((OWN, n, TOK, 2 * TOK), bf16),
            pltpu.VMEM((ch, TOK), f32),
            pltpu.VMEM((ch, TOK), f32),
            pltpu.VMEM((nt - 1, ch, TOK), bf16),
            pltpu.VMEM((nt - 1, ch, TOK), bf16),
            pltpu.VMEM((n, OWN, TOK), bf16),
            pltpu.VMEM((n, OWN, TOK), bf16),
            pltpu.VMEM((ch, TOK), f32),
            pltpu.VMEM((ch, TOK), f32),
            pltpu.VMEM((n, OWN, TOK), bf16),
            pltpu.VMEM((n, OWN, TOK), bf16),
            pltpu.VMEM((ch, TOK), f32),
            pltpu.VMEM((2 * ch, TOK), f32),
            pltpu.VMEM((2 * ch, TOK), bf16),
            pltpu.VMEM((2 * ch, TOK), bf16),
            pltpu.VMEM((nt, ny * nz, nc, gwr, TOK), bf16),
            pltpu.VMEM((TOK, every), bf16),
            pltpu.VMEM((every, cols), bf16),
            pltpu.VMEM((group, TOK, cols), bf16),
            pltpu.VMEM((group, ny * nz, gwr, TOK), bf16),
            pltpu.VMEM((tiles, ny * nz * gwr, wide), f32),
            pltpu.VMEM((tiles, ny - 1, tall, wide), bf16),
            pltpu.VMEM((tiles, ny - 1, tall, wide), bf16),
            pltpu.VMEM((tiles, gwr, wide), bf16),
            pltpu.VMEM((tiles, gwr, wide), bf16),
            pltpu.SemaphoreType.DMA((5,)),
            pltpu.SemaphoreType.DMA((5,)),
            pltpu.SemaphoreType.DMA((nt - 1,)),
            pltpu.SemaphoreType.DMA((nt - 1,)),
            pltpu.SemaphoreType.DMA((2, nt - 1, 2)),
            pltpu.SemaphoreType.DMA((2, nt - 1, 2)),
            pltpu.SemaphoreType.DMA,
            pltpu.SemaphoreType.DMA,
            pltpu.SemaphoreType.DMA,
            pltpu.SemaphoreType.DMA,
            pltpu.SemaphoreType.DMA((tiles,)),
            pltpu.SemaphoreType.DMA((tiles,)),
            pltpu.SemaphoreType.DMA((tiles,)),
            pltpu.SemaphoreType.DMA((tiles,)),
            pltpu.SemaphoreType.DMA,
        ],
        compiler_params=pltpu.CompilerParams(
            collective_id=0, has_side_effects=True, vmem_limit_bytes=56 * 1024 * 1024
        ),
    )(q, k, v, f, w, go)
    return place(results)


def solution(mesh, dims=(4, 4, 2, 2, 4)):
    return jax.shard_map(
        functools.partial(per_device, dims),
        mesh=mesh,
        in_specs=(
            P("ctx", "tp"),
            P("ctx", "tp"),
            P("ctx", "tp"),
            P("ctx", "tp"),
            P(None, "tp"),
            P("ctx", "tp"),
        ),
        out_specs=(P("ctx", "tp"),) * 6,
        check_vma=False,
    )
```

```python
import functools

import jax
import jax.numpy as jnp
from jax import lax
from jax.experimental import pallas as pl
from jax.experimental.pallas import tpu as pltpu
from jax.sharding import PartitionSpec as P

f32 = jnp.float32
bf16 = jnp.bfloat16
MESH = pl.DeviceIdType.MESH
OWN = 8
TOK = 128


def dot_nn(a, b):
    return lax.dot_general(a, b, (((1,), (0,)), ((), ())), preferred_element_type=f32)


def dot_nt(a, b):
    return lax.dot_general(a, b, (((1,), (1,)), ((), ())), preferred_element_type=f32)


def kernel(
    dims,
    qh_ref,
    kh_ref,
    vh_ref,
    fh_ref,
    wh_ref,
    goh_ref,
    outh_ref,
    gqh_ref,
    gkh_ref,
    gvh_ref,
    gfh_ref,
    gwh_ref,
    q_ref,
    k_ref,
    v_ref,
    f_ref,
    go_ref,
    out_ref,
    gq_ref,
    gk_ref,
    gv_ref,
    gf_ref,
    gw_ref,
    s1_ref,
    r1_ref,
    xf_ref,
    xpad_ref,
    gpad_ref,
    t_ref,
    qt_ref,
    gm_ref,
    ps_ref,
    pr_ref,
    gsb_ref,
    grb_ref,
    gr_ref,
    ys_ref,
    ysb_ref,
    yrb_ref,
    yr_ref,
    pqf_ref,
    pqs_ref,
    pqr_ref,
    mix_ref,
    ml_ref,
    w_ref,
    b_ref,
    a_ref,
    cf_ref,
    cs_ref,
    cr_ref,
    zs_ref,
    zr_ref,
    send_sem,
    recv_sem,
    tp_send,
    tp_recv,
    mx_send,
    mx_recv,
    b_send,
    b_recv,
    a_send,
    a_recv,
    c_send,
    c_recv,
    z_send,
    z_recv,
    local_sem,
):
    nx, ny, nz, nc, nt = dims
    n = nx * ny * nz * nc
    ch = OWN * n
    cols = go_ref.shape[1]
    gwr = gw_ref.shape[0]
    group = nx * nc
    me = lax.axis_index("ctx")
    tp = lax.axis_index("tp")
    core = me % nc
    zh = me // nc % nz
    yy = me // (nc * nz) % ny
    xx = me // (nc * nz * ny)
    slot = xx * nc + core

    row_id = lax.broadcasted_iota(jnp.int32, (TOK, TOK), 0)
    col_id = lax.broadcasted_iota(jnp.int32, (TOK, TOK), 1)
    eye = (row_id == col_id).astype(f32).astype(bf16)
    rev = (row_id + col_id == TOK - 1).astype(f32).astype(bf16)
    lower = col_id >= row_id

    def remote(src, dst, ssem, rsem, device):
        return pltpu.make_async_remote_copy(
            src_ref=src,
            dst_ref=dst,
            send_sem=ssem,
            recv_sem=rsem,
            device_id=device,
            device_id_type=MESH,
        )

    def wait_rows(ref, rows, sem):
        pltpu.make_async_copy(ref.at[pl.ds(0, rows)], ref.at[pl.ds(0, rows)], sem).wait()

    def each_peer(body):
        plane = n // nz
        place = me // (nz * nc) * nc + core

        def one(step, carry):
            level = (zh + nz - 1 - step // plane) % nz
            other = (place + step % plane) % plane
            body((other // nc * nz + level) * nc + other % nc)
            return carry

        lax.fori_loop(0, n - plane, one, 0)
        lax.fori_loop(n - plane + 1, n, one, 0)

    def spread8(src, dst, dst_block, index):
        def send(peer):
            remote(
                src.at[peer],
                dst.at[dst_block],
                send_sem.at[index],
                recv_sem.at[index],
                {"ctx": peer},
            ).start()

        each_peer(send)

    def spread(src, dst, size, src_block, dst_block, index):
        def send(peer):
            remote(
                src.at[pl.ds(pl.multiple_of(src_block(peer) * size, size), size)],
                dst.at[pl.ds(pl.multiple_of(dst_block * size, size), size)],
                send_sem.at[index],
                recv_sem.at[index],
                {"ctx": peer},
            ).start()

        each_peer(send)

    barrier = pltpu.get_barrier_semaphore()

    def greet(step, carry):
        pl.semaphore_signal(
            barrier, inc=1, device_id={"ctx": (me + step) % n}, device_id_type=MESH
        )
        return carry

    lax.fori_loop(1, n, greet, 0)
    for step in range(1, nt):
        pl.semaphore_signal(
            barrier, inc=1, device_id={"tp": (tp + step) % nt}, device_id_type=MESH
        )

    def bring(index, src, dst):
        copy = pltpu.make_async_copy(src, dst, local_sem.at[index])
        copy.start()
        return copy

    key_copy = bring(0, kh_ref, k_ref)
    value_copy = bring(1, vh_ref, v_ref)
    filter_copy = bring(2, fh_ref, f_ref)
    query_copy = bring(3, qh_ref, q_ref)
    grad_copy = bring(4, goh_ref, go_ref)
    weight_copy = bring(5, wh_ref, w_ref)
    key_copy.wait()
    value_copy.wait()
    filter_copy.wait()
    query_copy.wait()

    for j in range(ch // TOK):
        lanes = pl.ds(j * TOK, TOK)
        gated = (k_ref[:, lanes].astype(f32) * v_ref[:, lanes].astype(f32)).astype(bf16)
        gated_t = dot_nt(eye, gated).reshape(TOK // OWN, OWN, TOK)
        filter_t = dot_nt(eye, f_ref[:, lanes].astype(bf16)).reshape(TOK // OWN, OWN, TOK)
        both = jnp.concatenate([gated_t, filter_t], axis=1)
        s1_ref[pl.ds(2 * j * TOK, 2 * TOK), :] = both.reshape(2 * TOK, TOK).astype(bf16)
        qt_ref[pl.ds(j * TOK, TOK), :] = dot_nt(eye, q_ref[:, lanes])

    pl.semaphore_wait(barrier, n - 1 + nt - 1)
    spread(s1_ref, r1_ref, 2 * OWN, lambda peer: peer, me, 0)

    part = min(ch, 512)
    grad_copy.wait()
    weight_copy.wait()

    def partial(target, write):
        def rows(i, carry):
            start = pl.multiple_of(target * ch + i * part, part)
            write(
                pl.ds(pl.multiple_of(i * part, part), part),
                dot_nt(w_ref[pl.ds(start, part), :], go_ref[...]),
            )
            return carry

        lax.fori_loop(0, ch // part, rows, 0)

    for step in range(1, nt):

        def put(rows, value, step=step):
            ps_ref[step - 1, rows, :] = value.astype(bf16)

        partial((tp + step) % nt, put)

    def put_own(rows, value):
        gm_ref[rows, :] = value

    partial(tp, put_own)

    wait_rows(r1_ref, (n - 1) * 2 * OWN, recv_sem.at[0])
    mine = pl.ds(pl.multiple_of(me * 2 * OWN, 2 * OWN), 2 * OWN)
    for step in range(1, nt):
        remote(
            ps_ref.at[step - 1],
            pr_ref.at[step - 1],
            tp_send.at[step - 1],
            tp_recv.at[step - 1],
            {"tp": (tp + step) % nt},
        ).start()

    def along(step):
        return remote(
            go_ref,
            b_ref.at[slot],
            b_send,
            b_recv,
            {"ctx": (((xx + step) % nx * ny + yy) * nz + zh) * nc + core},
        )

    for step in range(1, nx):
        along(step).start()
    r1_ref[mine, :] = s1_ref[mine, :]
    xf_ref[...] = r1_ref[...].astype(f32)

    def toeplitz(c, first, lanes):
        def block(d, before):
            line = xf_ref[pl.ds(d * 2 * OWN + first + c, 1), :]
            now = pltpu.roll(
                jnp.broadcast_to(line, (TOK, TOK)), 0, 1, stride=1, stride_axis=0
            )
            t_ref[c, d, :, lanes] = jnp.where(lower, now, before).astype(bf16)
            return now

        lax.fori_loop(0, n, block, jnp.zeros((TOK, TOK), f32), unroll=n)

    def convolve(pad, c, lanes, width):
        left = jnp.concatenate(
            [pad[c, pl.ds(n - i, n), :].astype(bf16) for i in range(n)], axis=1
        )
        return dot_nn(left, t_ref[c, :, :, lanes].reshape(n * TOK, width))

    def forward(c, carry):
        xpad_ref[c, pl.ds(0, n), :] = jnp.zeros((n, TOK), f32)
        xpad_ref[c, pl.ds(n, n), :] = xf_ref[pl.ds(c, n, stride=2 * OWN), :]
        toeplitz(c, OWN, pl.ds(0, TOK))
        ys_ref[pl.ds(c, n, stride=OWN), :] = convolve(xpad_ref, c, pl.ds(0, TOK), TOK)
        return carry

    lax.fori_loop(0, OWN, forward, 0)
    ysb_ref[...] = ys_ref[...].reshape(n, OWN, TOK).astype(bf16)
    spread8(ysb_ref, yrb_ref, me, 2)

    for step in range(1, nt):
        remote(
            ps_ref.at[step - 1],
            pr_ref.at[step - 1],
            tp_send.at[step - 1],
            tp_recv.at[step - 1],
            {"tp": (tp + step) % nt},
        ).wait_recv()

    def sum_rows(i, carry):
        rows = pl.ds(pl.multiple_of(i * TOK, TOK), TOK)
        total = gm_ref[rows, :]
        for step in range(1, nt):
            total = total + pr_ref[step - 1, rows, :].astype(f32)
        gm_ref[rows, :] = total
        back = dot_nn((total * qt_ref[rows, :]).astype(bf16), rev)
        gsb_ref[pl.ds(i * (TOK // OWN), TOK // OWN)] = back.reshape(
            TOK // OWN, OWN, TOK
        ).astype(bf16)
        return carry

    lax.fori_loop(0, ch // TOK, sum_rows, 0)
    spread8(gsb_ref, grb_ref, n - 1 - me, 1)

    wait_rows(yrb_ref, n - 1, recv_sem.at[2])
    yrb_ref[me] = ysb_ref[me]
    yr_ref[...] = yrb_ref[...].astype(f32).reshape(ch, TOK)
    blocks = ny * nz
    per = TOK // (nc * gwr)

    def mix(i, carry):
        rows = pl.ds(pl.multiple_of(i * TOK, TOK), TOK)
        mixed = (qt_ref[rows, :] * yr_ref[rows, :]).astype(bf16)
        mix_ref[tp, pl.ds(i * per, per)] = mixed.reshape(per, nc, gwr, TOK)
        return carry

    lax.fori_loop(0, ch // TOK, mix, 0)

    half = blocks // 2

    def pass_on(source, way, hop, piece):
        rows = mix_ref.at[source, pl.ds(piece * half, half)]
        return remote(
            rows,
            rows,
            mx_send.at[way, hop, piece],
            mx_recv.at[way, hop, piece],
            {"tp": jnp.clip(tp + (1 - 2 * way), 0, nt - 1)},
        )

    def has_next(way):
        return tp < nt - 1 if way == 0 else tp > 0

    def has_hop(way, hop):
        return tp >= hop if way == 0 else tp + hop < nt

    for piece in range(2):
        for way in range(2):

            @pl.when(has_next(way))
            def _(way=way, piece=piece):
                pass_on(tp, way, 0, piece).start()

    def feed(source, piece):
        part_rows = pl.ds(piece * half, half)
        for core_step in range(nc):
            to_core = (core + core_step) % nc
            copy = remote(
                mix_ref.at[source, part_rows, to_core],
                a_ref.at[slot, part_rows],
                a_send,
                a_recv,
                {"ctx": ((source * ny + yy) * nz + zh) * nc + to_core},
            )
            if core_step == 0:

                @pl.when(xx != source)
                def _(copy=copy):
                    copy.start()

            else:
                copy.start()

    def other_blocks(c, carry):
        toeplitz(c, 0, pl.ds(TOK, TOK))
        return carry

    feed(tp, 0)
    feed(tp, 1)

    wait_rows(b_ref, nx - 1, b_recv)
    b_ref[slot] = go_ref[...]

    def to_core(step, x_step):
        block = b_ref.at[(xx + x_step) % nx * nc + core]
        return remote(
            block,
            block,
            send_sem.at[4],
            recv_sem.at[4],
            {"ctx": me - core + (core + step) % nc},
        )

    for step in range(1, nc):
        for x_step in range(nx):
            to_core(step, x_step).start()

    done = 0
    for hop in range(1, nt):
        until = OWN * hop // (nt - 1)
        lax.fori_loop(done, until, other_blocks, 0)
        done = until
        for piece in range(2):
            for way in range(2):

                @pl.when(has_hop(way, hop))
                def _(way=way, hop=hop, piece=piece):
                    source = tp - hop * (1 - 2 * way)
                    pass_on(source, way, hop - 1, piece).wait_recv()
                    if hop < nt - 1:

                        @pl.when(has_next(way))
                        def _():
                            pass_on(source, way, hop, piece).start()

                    feed(source, piece)

    wait_rows(grb_ref, n - 1, recv_sem.at[1])
    grb_ref[n - 1 - me] = gsb_ref[me]
    gr_ref[...] = grb_ref[...].astype(f32).reshape(ch, TOK)

    def backward(c, carry):
        gpad_ref[c, pl.ds(0, n), :] = jnp.zeros((n, TOK), f32)
        gpad_ref[c, pl.ds(n, n), :] = gr_ref[pl.ds(c, n, stride=OWN), :]
        acc = convolve(gpad_ref, c, pl.ds(0, 2 * TOK), 2 * TOK)
        pqf_ref[pl.ds(c, n, stride=2 * OWN), :] = acc[:, :TOK]
        pqf_ref[pl.ds(OWN + c, n, stride=2 * OWN), :] = acc[:, TOK:]
        return carry

    lax.fori_loop(0, OWN, backward, 0)
    pqs_ref[...] = pqf_ref[...].astype(bf16)

    if nc > 1:
        wait_rows(b_ref, nx * (nc - 1), recv_sem.at[4])
    wait_rows(a_ref, group - 1, a_recv)
    a_ref[slot] = mix_ref[xx, :, core]

    wide = min(cols, 256)
    tiles = cols // wide
    tall = nz * gwr

    def send_tile(i, y_step):
        other = (yy + y_step) % ny
        return remote(
            cs_ref.at[i, y_step - 1],
            cr_ref.at[i, y_step - 1],
            c_send.at[i],
            c_recv.at[i],
            {"ctx": ((xx * ny + other) * nz + zh) * nc + core},
        )

    def weight(i, carry):
        columns = pl.ds(pl.multiple_of(i * wide, wide), wide)
        acc = jnp.zeros((blocks * gwr, wide), f32)
        for source in range(group):
            left = a_ref[source].reshape(blocks * gwr, TOK)
            acc = acc + dot_nn(left, b_ref[source, :, columns])
        cf_ref[i] = acc
        for y_step in range(1, ny):
            other = (yy + y_step) % ny
            rows = pl.ds(pl.multiple_of(other * tall, tall), tall)
            cs_ref[i, y_step - 1] = cf_ref[i, rows, :].astype(bf16)
            send_tile(i, y_step).start()
        return carry

    lax.fori_loop(0, tiles, weight, 0)

    spread(pqs_ref, pqr_ref, 2 * OWN, lambda peer: n - 1 - peer, me, 3)

    far = (zh + 1) % nz

    def across(i):
        return remote(
            zs_ref.at[i],
            zr_ref.at[i],
            z_send.at[i],
            z_recv.at[i],
            {"ctx": ((xx * ny + yy) * nz + far) * nc + core},
        )

    def over_y(i, carry):
        pltpu.make_async_copy(cr_ref.at[i], cr_ref.at[i], c_recv.at[i]).wait()

        def total(level):
            rows = pl.ds(pl.multiple_of(level * gwr, gwr), gwr)
            value = cf_ref[i, pl.ds(pl.multiple_of(yy * tall + level * gwr, gwr), gwr), :]
            for y_step in range(1, ny):
                value = value + cr_ref[i, y_step - 1, rows, :].astype(f32)
            return value

        zs_ref[i] = total(far).astype(bf16)
        across(i).start()
        gw_ref[:, pl.ds(pl.multiple_of(i * wide, wide), wide)] = total(zh)
        return carry

    lax.fori_loop(0, tiles, over_y, 0)

    def turn(source, carry):
        left = dot_nt(eye, mix_ref[source].reshape(ch, TOK)).astype(bf16)
        ml_ref[:, pl.ds(pl.multiple_of(source * ch, ch), ch)] = left
        return carry

    lax.fori_loop(0, nt, turn, 0)

    def project(i, carry):
        columns = pl.ds(pl.multiple_of(i * wide, wide), wide)
        out_ref[:, columns] = dot_nn(ml_ref[...], w_ref[:, columns]).astype(bf16)
        return carry

    lax.fori_loop(0, tiles, project, 0)

    def query(j, carry):
        rows = pl.ds(pl.multiple_of(j * TOK, TOK), TOK)
        grad = (gm_ref[rows, :] * yr_ref[rows, :]).astype(bf16)
        gq_ref[:, rows] = dot_nt(eye, grad).astype(bf16)
        return carry

    lax.fori_loop(0, ch // TOK, query, 0)
    leaving = [bring(6, out_ref, outh_ref), bring(7, gq_ref, gqh_ref)]
    wait_rows(pqr_ref, (n - 1) * 2 * OWN, recv_sem.at[3])
    back = pl.ds(pl.multiple_of((n - 1 - me) * 2 * OWN, 2 * OWN), 2 * OWN)
    pqr_ref[mine, :] = pqs_ref[back, :]

    def finish(j, carry):
        lanes = pl.ds(pl.multiple_of(j * TOK, TOK), TOK)
        both = pqr_ref[pl.ds(pl.multiple_of(2 * j * TOK, TOK), 2 * TOK), :].astype(f32)
        both = both.reshape(TOK // OWN, 2 * OWN, TOK)
        grad_gated = dot_nt(rev, both[:, :OWN].reshape(TOK, TOK).astype(bf16))
        gf_ref[:, lanes] = dot_nt(rev, both[:, OWN:].reshape(TOK, TOK).astype(bf16))
        gk_ref[:, lanes] = (grad_gated * v_ref[:, lanes].astype(f32)).astype(bf16)
        gv_ref[:, lanes] = (grad_gated * k_ref[:, lanes].astype(f32)).astype(bf16)
        return carry

    lax.fori_loop(0, ch // TOK, finish, 0)

    leaving += [
        bring(8, gk_ref, gkh_ref),
        bring(9, gv_ref, gvh_ref),
        bring(10, gf_ref, gfh_ref),
    ]

    def over_z(i, carry):
        across(i).wait_recv()
        columns = pl.ds(pl.multiple_of(i * wide, wide), wide)
        gw_ref[:, columns] = gw_ref[:, columns] + zr_ref[i].astype(f32)
        return carry

    lax.fori_loop(0, tiles, over_z, 0)

    leaving.append(bring(11, gw_ref, gwh_ref))

    for copy in leaving:
        copy.wait()
    wait_rows(s1_ref, (n - 1) * 2 * OWN, send_sem.at[0])
    wait_rows(gsb_ref, n - 1, send_sem.at[1])
    wait_rows(ysb_ref, n - 1, send_sem.at[2])
    wait_rows(pqs_ref, (n - 1) * 2 * OWN, send_sem.at[3])
    wait_rows(b_ref, nx - 1, b_send)
    if nc > 1:
        wait_rows(b_ref, nx * (nc - 1), send_sem.at[4])

    wait_rows(a_ref, group - 1, a_send)

    def left_tile(i, carry):
        pltpu.make_async_copy(cs_ref.at[i], cs_ref.at[i], c_send.at[i]).wait()
        across(i).wait_send()
        return carry

    lax.fori_loop(0, tiles, left_tile, 0)
    for step in range(1, nt):
        peer = {"tp": (tp + step) % nt}
        remote(
            ps_ref.at[step - 1],
            pr_ref.at[step - 1],
            tp_send.at[step - 1],
            tp_recv.at[step - 1],
            peer,
        ).wait_send()
    for hop in range(nt - 1):
        for piece in range(2):
            for way in range(2):

                @pl.when(has_next(way) & has_hop(way, hop))
                def _(way=way, hop=hop, piece=piece):
                    pass_on(tp - hop * (1 - 2 * way), way, hop, piece).wait_send()


def place_kernel(*refs):
    copies = [
        pltpu.make_async_copy(refs[i], refs[6 + i], refs[12].at[i]) for i in range(6)
    ]
    for copy in copies:
        copy.start()
    for copy in copies:
        copy.wait()


def place(arrays):
    anywhere = pl.BlockSpec(memory_space=pl.ANY)
    return pl.pallas_call(
        place_kernel,
        out_shape=tuple(jax.ShapeDtypeStruct(a.shape, a.dtype) for a in arrays),
        in_specs=[anywhere] * 6,
        out_specs=[pl.BlockSpec(memory_space=pltpu.VMEM)] * 6,
        scratch_shapes=[pltpu.SemaphoreType.DMA((6,))],
        compiler_params=pltpu.CompilerParams(vmem_limit_bytes=60 * 1024 * 1024),
    )(*arrays)


def per_device(dims, q, k, v, f, w, go):
    nx, ny, nz, nc, nt = dims
    n = nx * ny * nz * nc
    ch = OWN * n
    every = ch * nt
    cols = go.shape[1]
    gwr = every // n
    group = nx * nc
    tall = nz * gwr
    wide = min(cols, 256)
    tiles = cols // wide
    anywhere = pl.BlockSpec(memory_space=pl.ANY)
    results = pl.pallas_call(
        functools.partial(kernel, dims),
        out_shape=(
            jax.ShapeDtypeStruct((TOK, cols), bf16),
            jax.ShapeDtypeStruct((TOK, ch), bf16),
            jax.ShapeDtypeStruct((TOK, ch), bf16),
            jax.ShapeDtypeStruct((TOK, ch), bf16),
            jax.ShapeDtypeStruct((TOK, ch), f32),
            jax.ShapeDtypeStruct((gwr, cols), f32),
        ),
        in_specs=[anywhere] * 6,
        out_specs=[anywhere] * 6,
        scratch_shapes=[
            pltpu.VMEM((TOK, ch), bf16),
            pltpu.VMEM((TOK, ch), bf16),
            pltpu.VMEM((TOK, ch), bf16),
            pltpu.VMEM((TOK, ch), f32),
            pltpu.VMEM((TOK, cols), bf16),
            pltpu.VMEM((TOK, cols), bf16),
            pltpu.VMEM((TOK, ch), bf16),
            pltpu.VMEM((TOK, ch), bf16),
            pltpu.VMEM((TOK, ch), bf16),
            pltpu.VMEM((TOK, ch), f32),
            pltpu.VMEM((gwr, cols), f32),
            pltpu.VMEM((2 * ch, TOK), bf16),
            pltpu.VMEM((2 * ch, TOK), bf16),
            pltpu.VMEM((2 * ch, TOK), f32),
            pltpu.VMEM((OWN, 2 * n, TOK), f32),
            pltpu.VMEM((OWN, 2 * n, TOK), f32),
            pltpu.VMEM((OWN, n, TOK, 2 * TOK), bf16),
            pltpu.VMEM((ch, TOK), f32),
            pltpu.VMEM((ch, TOK), f32),
            pltpu.VMEM((nt - 1, ch, TOK), bf16),
            pltpu.VMEM((nt - 1, ch, TOK), bf16),
            pltpu.VMEM((n, OWN, TOK), bf16),
            pltpu.VMEM((n, OWN, TOK), bf16),
            pltpu.VMEM((ch, TOK), f32),
            pltpu.VMEM((ch, TOK), f32),
            pltpu.VMEM((n, OWN, TOK), bf16),
            pltpu.VMEM((n, OWN, TOK), bf16),
            pltpu.VMEM((ch, TOK), f32),
            pltpu.VMEM((2 * ch, TOK), f32),
            pltpu.VMEM((2 * ch, TOK), bf16),
            pltpu.VMEM((2 * ch, TOK), bf16),
            pltpu.VMEM((nt, ny * nz, nc, gwr, TOK), bf16),
            pltpu.VMEM((TOK, every), bf16),
            pltpu.VMEM((every, cols), bf16),
            pltpu.VMEM((group, TOK, cols), bf16),
            pltpu.VMEM((group, ny * nz, gwr, TOK), bf16),
            pltpu.VMEM((tiles, ny * nz * gwr, wide), f32),
            pltpu.VMEM((tiles, ny - 1, tall, wide), bf16),
            pltpu.VMEM((tiles, ny - 1, tall, wide), bf16),
            pltpu.VMEM((tiles, gwr, wide), bf16),
            pltpu.VMEM((tiles, gwr, wide), bf16),
            pltpu.SemaphoreType.DMA((5,)),
            pltpu.SemaphoreType.DMA((5,)),
            pltpu.SemaphoreType.DMA((nt - 1,)),
            pltpu.SemaphoreType.DMA((nt - 1,)),
            pltpu.SemaphoreType.DMA((2, nt - 1, 2)),
            pltpu.SemaphoreType.DMA((2, nt - 1, 2)),
            pltpu.SemaphoreType.DMA,
            pltpu.SemaphoreType.DMA,
            pltpu.SemaphoreType.DMA,
            pltpu.SemaphoreType.DMA,
            pltpu.SemaphoreType.DMA((tiles,)),
            pltpu.SemaphoreType.DMA((tiles,)),
            pltpu.SemaphoreType.DMA((tiles,)),
            pltpu.SemaphoreType.DMA((tiles,)),
            pltpu.SemaphoreType.DMA((12,)),
        ],
        compiler_params=pltpu.CompilerParams(
            collective_id=0, has_side_effects=True, vmem_limit_bytes=56 * 1024 * 1024
        ),
    )(q, k, v, f, w, go)
    return place(results)


def solution(mesh, dims=(4, 4, 2, 2, 4)):
    return jax.shard_map(
        functools.partial(per_device, dims),
        mesh=mesh,
        in_specs=(
            P("ctx", "tp"),
            P("ctx", "tp"),
            P("ctx", "tp"),
            P("ctx", "tp"),
            P(None, "tp"),
            P("ctx", "tp"),
        ),
        out_specs=(P("ctx", "tp"),) * 6,
        check_vma=False,
    )
```

```python
import functools

import jax
import jax.numpy as jnp
from jax import lax
from jax.experimental import pallas as pl
from jax.experimental.pallas import tpu as pltpu
from jax.sharding import PartitionSpec as P

f32 = jnp.float32
bf16 = jnp.bfloat16
MESH = pl.DeviceIdType.MESH
OWN = 8
TOK = 128


def dot_nn(a, b):
    return lax.dot_general(a, b, (((1,), (0,)), ((), ())), preferred_element_type=f32)


def dot_nt(a, b):
    return lax.dot_general(a, b, (((1,), (1,)), ((), ())), preferred_element_type=f32)


def kernel(
    dims,
    qh_ref,
    kh_ref,
    vh_ref,
    fh_ref,
    wh_ref,
    goh_ref,
    outh_ref,
    gqh_ref,
    gkh_ref,
    gvh_ref,
    gfh_ref,
    gwh_ref,
    q_ref,
    k_ref,
    v_ref,
    f_ref,
    go_ref,
    out_ref,
    gq_ref,
    gk_ref,
    gv_ref,
    gf_ref,
    gw_ref,
    s1_ref,
    r1_ref,
    xf_ref,
    xpad_ref,
    gpad_ref,
    t_ref,
    qt_ref,
    gm_ref,
    ps_ref,
    pr_ref,
    gsb_ref,
    grb_ref,
    gr_ref,
    ys_ref,
    ysb_ref,
    yrb_ref,
    yr_ref,
    pqf_ref,
    pqs_ref,
    pqr_ref,
    mix_ref,
    ml_ref,
    w_ref,
    b_ref,
    a_ref,
    cf_ref,
    cs_ref,
    cr_ref,
    zs_ref,
    zr_ref,
    send_sem,
    recv_sem,
    tp_send,
    tp_recv,
    mx_send,
    mx_recv,
    b_send,
    b_recv,
    a_send,
    a_recv,
    c_send,
    c_recv,
    z_send,
    z_recv,
    local_sem,
):
    nx, ny, nz, nc, nt = dims
    n = nx * ny * nz * nc
    ch = OWN * n
    cols = go_ref.shape[1]
    gwr = gw_ref.shape[0]
    group = nx * nc
    me = lax.axis_index("ctx")
    tp = lax.axis_index("tp")
    core = me % nc
    zh = me // nc % nz
    yy = me // (nc * nz) % ny
    xx = me // (nc * nz * ny)
    slot = xx * nc + core

    row_id = lax.broadcasted_iota(jnp.int32, (TOK, TOK), 0)
    col_id = lax.broadcasted_iota(jnp.int32, (TOK, TOK), 1)
    eye = (row_id == col_id).astype(f32).astype(bf16)
    rev = (row_id + col_id == TOK - 1).astype(f32).astype(bf16)
    lower = col_id >= row_id

    def remote(src, dst, ssem, rsem, device):
        return pltpu.make_async_remote_copy(
            src_ref=src,
            dst_ref=dst,
            send_sem=ssem,
            recv_sem=rsem,
            device_id=device,
            device_id_type=MESH,
        )

    def wait_rows(ref, rows, sem):
        pltpu.make_async_copy(ref.at[pl.ds(0, rows)], ref.at[pl.ds(0, rows)], sem).wait()

    def each_peer(body):
        plane = n // nz
        place = me // (nz * nc) * nc + core

        def one(step, carry):
            level = (zh + nz - 1 - step // plane) % nz
            other = (place + step % plane) % plane
            body((other // nc * nz + level) * nc + other % nc)
            return carry

        lax.fori_loop(0, n - plane, one, 0)
        lax.fori_loop(n - plane + 1, n, one, 0)

    def spread8(src, dst, dst_block, index):
        def send(peer):
            remote(
                src.at[peer],
                dst.at[dst_block],
                send_sem.at[index],
                recv_sem.at[index],
                {"ctx": peer},
            ).start()

        each_peer(send)

    def spread(src, dst, size, src_block, dst_block, index):
        def send(peer):
            remote(
                src.at[pl.ds(pl.multiple_of(src_block(peer) * size, size), size)],
                dst.at[pl.ds(pl.multiple_of(dst_block * size, size), size)],
                send_sem.at[index],
                recv_sem.at[index],
                {"ctx": peer},
            ).start()

        each_peer(send)

    barrier = pltpu.get_barrier_semaphore()

    def greet(step, carry):
        pl.semaphore_signal(
            barrier, inc=1, device_id={"ctx": (me + step) % n}, device_id_type=MESH
        )
        return carry

    lax.fori_loop(1, n, greet, 0)
    for step in range(1, nt):
        pl.semaphore_signal(
            barrier, inc=1, device_id={"tp": (tp + step) % nt}, device_id_type=MESH
        )

    def bring(index, src, dst):
        copy = pltpu.make_async_copy(src, dst, local_sem.at[index])
        copy.start()
        return copy

    key_copy = bring(0, kh_ref, k_ref)
    value_copy = bring(1, vh_ref, v_ref)
    filter_copy = bring(2, fh_ref, f_ref)
    query_copy = bring(3, qh_ref, q_ref)
    grad_copy = bring(4, goh_ref, go_ref)
    weight_copy = bring(5, wh_ref, w_ref)
    key_copy.wait()
    value_copy.wait()
    filter_copy.wait()
    query_copy.wait()

    for j in range(ch // TOK):
        lanes = pl.ds(j * TOK, TOK)
        gated = (k_ref[:, lanes].astype(f32) * v_ref[:, lanes].astype(f32)).astype(bf16)
        gated_t = dot_nt(eye, gated).reshape(TOK // OWN, OWN, TOK)
        filter_t = dot_nt(eye, f_ref[:, lanes].astype(bf16)).reshape(TOK // OWN, OWN, TOK)
        both = jnp.concatenate([gated_t, filter_t], axis=1)
        s1_ref[pl.ds(2 * j * TOK, 2 * TOK), :] = both.reshape(2 * TOK, TOK).astype(bf16)
        qt_ref[pl.ds(j * TOK, TOK), :] = dot_nt(eye, q_ref[:, lanes])

    pl.semaphore_wait(barrier, n - 1 + nt - 1)
    spread(s1_ref, r1_ref, 2 * OWN, lambda peer: peer, me, 0)

    part = min(ch, 512)
    grad_copy.wait()
    weight_copy.wait()

    def partial(target, write):
        def rows(i, carry):
            start = pl.multiple_of(target * ch + i * part, part)
            write(
                pl.ds(pl.multiple_of(i * part, part), part),
                dot_nt(w_ref[pl.ds(start, part), :], go_ref[...]),
            )
            return carry

        lax.fori_loop(0, ch // part, rows, 0)

    for step in range(1, nt):

        def put(rows, value, step=step):
            ps_ref[step - 1, rows, :] = value.astype(bf16)

        partial((tp + step) % nt, put)

    def put_own(rows, value):
        gm_ref[rows, :] = value

    partial(tp, put_own)

    wait_rows(r1_ref, (n - 1) * 2 * OWN, recv_sem.at[0])
    mine = pl.ds(pl.multiple_of(me * 2 * OWN, 2 * OWN), 2 * OWN)
    for step in range(1, nt):
        remote(
            ps_ref.at[step - 1],
            pr_ref.at[step - 1],
            tp_send.at[step - 1],
            tp_recv.at[step - 1],
            {"tp": (tp + step) % nt},
        ).start()

    def along(step):
        return remote(
            go_ref,
            b_ref.at[slot],
            b_send,
            b_recv,
            {"ctx": (((xx + step) % nx * ny + yy) * nz + zh) * nc + core},
        )

    r1_ref[mine, :] = s1_ref[mine, :]
    xf_ref[...] = r1_ref[...].astype(f32)

    def toeplitz(c, first, lanes):
        def block(d, before):
            line = xf_ref[pl.ds(d * 2 * OWN + first + c, 1), :]
            now = pltpu.roll(
                jnp.broadcast_to(line, (TOK, TOK)), 0, 1, stride=1, stride_axis=0
            )
            t_ref[c, d, :, lanes] = jnp.where(lower, now, before).astype(bf16)
            return now

        lax.fori_loop(0, n, block, jnp.zeros((TOK, TOK), f32), unroll=n)

    def convolve(pad, c, lanes, width):
        left = jnp.concatenate(
            [pad[c, pl.ds(n - i, n), :].astype(bf16) for i in range(n)], axis=1
        )
        return dot_nn(left, t_ref[c, :, :, lanes].reshape(n * TOK, width))

    def forward(c, carry):
        xpad_ref[c, pl.ds(0, n), :] = jnp.zeros((n, TOK), f32)
        xpad_ref[c, pl.ds(n, n), :] = xf_ref[pl.ds(c, n, stride=2 * OWN), :]
        toeplitz(c, OWN, pl.ds(0, TOK))
        ys_ref[pl.ds(c, n, stride=OWN), :] = convolve(xpad_ref, c, pl.ds(0, TOK), TOK)
        return carry

    lax.fori_loop(0, OWN, forward, 0)
    ysb_ref[...] = ys_ref[...].reshape(n, OWN, TOK).astype(bf16)
    spread8(ysb_ref, yrb_ref, me, 2)
    for step in range(1, nx):
        along(step).start()

    for step in range(1, nt):
        remote(
            ps_ref.at[step - 1],
            pr_ref.at[step - 1],
            tp_send.at[step - 1],
            tp_recv.at[step - 1],
            {"tp": (tp + step) % nt},
        ).wait_recv()

    def sum_rows(i, carry):
        rows = pl.ds(pl.multiple_of(i * TOK, TOK), TOK)
        total = gm_ref[rows, :]
        for step in range(1, nt):
            total = total + pr_ref[step - 1, rows, :].astype(f32)
        gm_ref[rows, :] = total
        back = dot_nn((total * qt_ref[rows, :]).astype(bf16), rev)
        gsb_ref[pl.ds(i * (TOK // OWN), TOK // OWN)] = back.reshape(
            TOK // OWN, OWN, TOK
        ).astype(bf16)
        return carry

    lax.fori_loop(0, ch // TOK, sum_rows, 0)
    spread8(gsb_ref, grb_ref, n - 1 - me, 1)

    wait_rows(yrb_ref, n - 1, recv_sem.at[2])
    yrb_ref[me] = ysb_ref[me]
    yr_ref[...] = yrb_ref[...].astype(f32).reshape(ch, TOK)
    blocks = ny * nz
    per = TOK // (nc * gwr)

    def mix(i, carry):
        rows = pl.ds(pl.multiple_of(i * TOK, TOK), TOK)
        mixed = (qt_ref[rows, :] * yr_ref[rows, :]).astype(bf16)
        mix_ref[tp, pl.ds(i * per, per)] = mixed.reshape(per, nc, gwr, TOK)
        return carry

    lax.fori_loop(0, ch // TOK, mix, 0)

    half = blocks // 2

    def pass_on(source, way, hop, piece):
        rows = mix_ref.at[source, pl.ds(piece * half, half)]
        return remote(
            rows,
            rows,
            mx_send.at[way, hop, piece],
            mx_recv.at[way, hop, piece],
            {"tp": jnp.clip(tp + (1 - 2 * way), 0, nt - 1)},
        )

    def has_next(way):
        return tp < nt - 1 if way == 0 else tp > 0

    def has_hop(way, hop):
        return tp >= hop if way == 0 else tp + hop < nt

    for piece in range(2):
        for way in range(2):

            @pl.when(has_next(way))
            def _(way=way, piece=piece):
                pass_on(tp, way, 0, piece).start()

    def feed(source, piece):
        part_rows = pl.ds(piece * half, half)
        for core_step in range(nc):
            to_core = (core + core_step) % nc
            copy = remote(
                mix_ref.at[source, part_rows, to_core],
                a_ref.at[slot, part_rows],
                a_send,
                a_recv,
                {"ctx": ((source * ny + yy) * nz + zh) * nc + to_core},
            )
            if core_step == 0:

                @pl.when(xx != source)
                def _(copy=copy):
                    copy.start()

            else:
                copy.start()

    def other_blocks(c, carry):
        toeplitz(c, 0, pl.ds(TOK, TOK))
        return carry

    feed(tp, 0)
    feed(tp, 1)

    wait_rows(b_ref, nx - 1, b_recv)
    b_ref[slot] = go_ref[...]

    def to_core(step, x_step):
        block = b_ref.at[(xx + x_step) % nx * nc + core]
        return remote(
            block,
            block,
            send_sem.at[4],
            recv_sem.at[4],
            {"ctx": me - core + (core + step) % nc},
        )

    for step in range(1, nc):
        for x_step in range(nx):
            to_core(step, x_step).start()

    done = 0
    for hop in range(1, nt):
        until = OWN * hop // (nt - 1)
        lax.fori_loop(done, until, other_blocks, 0)
        done = until
        for piece in range(2):
            for way in range(2):

                @pl.when(has_hop(way, hop))
                def _(way=way, hop=hop, piece=piece):
                    source = tp - hop * (1 - 2 * way)
                    pass_on(source, way, hop - 1, piece).wait_recv()
                    if hop < nt - 1:

                        @pl.when(has_next(way))
                        def _():
                            pass_on(source, way, hop, piece).start()

                    feed(source, piece)

    wait_rows(grb_ref, n - 1, recv_sem.at[1])
    grb_ref[n - 1 - me] = gsb_ref[me]
    gr_ref[...] = grb_ref[...].astype(f32).reshape(ch, TOK)

    def backward(c, carry):
        gpad_ref[c, pl.ds(0, n), :] = jnp.zeros((n, TOK), f32)
        gpad_ref[c, pl.ds(n, n), :] = gr_ref[pl.ds(c, n, stride=OWN), :]
        acc = convolve(gpad_ref, c, pl.ds(0, 2 * TOK), 2 * TOK)
        pqf_ref[pl.ds(c, n, stride=2 * OWN), :] = acc[:, :TOK]
        pqf_ref[pl.ds(OWN + c, n, stride=2 * OWN), :] = acc[:, TOK:]
        return carry

    lax.fori_loop(0, OWN, backward, 0)
    pqs_ref[...] = pqf_ref[...].astype(bf16)

    if nc > 1:
        wait_rows(b_ref, nx * (nc - 1), recv_sem.at[4])
    wait_rows(a_ref, group - 1, a_recv)
    a_ref[slot] = mix_ref[xx, :, core]

    wide = min(cols, 256)
    tiles = cols // wide
    tall = nz * gwr

    def send_tile(i, y_step):
        other = (yy + y_step) % ny
        return remote(
            cs_ref.at[i, y_step - 1],
            cr_ref.at[i, y_step - 1],
            c_send.at[i],
            c_recv.at[i],
            {"ctx": ((xx * ny + other) * nz + zh) * nc + core},
        )

    def weight(i, carry):
        columns = pl.ds(pl.multiple_of(i * wide, wide), wide)
        acc = jnp.zeros((blocks * gwr, wide), f32)
        for source in range(group):
            left = a_ref[source].reshape(blocks * gwr, TOK)
            acc = acc + dot_nn(left, b_ref[source, :, columns])
        cf_ref[i] = acc
        for y_step in range(1, ny):
            other = (yy + y_step) % ny
            rows = pl.ds(pl.multiple_of(other * tall, tall), tall)
            cs_ref[i, y_step - 1] = cf_ref[i, rows, :].astype(bf16)
            send_tile(i, y_step).start()
        return carry

    lax.fori_loop(0, tiles, weight, 0)

    spread(pqs_ref, pqr_ref, 2 * OWN, lambda peer: n - 1 - peer, me, 3)

    far = (zh + 1) % nz

    def across(i):
        return remote(
            zs_ref.at[i],
            zr_ref.at[i],
            z_send.at[i],
            z_recv.at[i],
            {"ctx": ((xx * ny + yy) * nz + far) * nc + core},
        )

    def over_y(i, carry):
        pltpu.make_async_copy(cr_ref.at[i], cr_ref.at[i], c_recv.at[i]).wait()

        def total(level):
            rows = pl.ds(pl.multiple_of(level * gwr, gwr), gwr)
            value = cf_ref[i, pl.ds(pl.multiple_of(yy * tall + level * gwr, gwr), gwr), :]
            for y_step in range(1, ny):
                value = value + cr_ref[i, y_step - 1, rows, :].astype(f32)
            return value

        zs_ref[i] = total(far).astype(bf16)
        across(i).start()
        gw_ref[:, pl.ds(pl.multiple_of(i * wide, wide), wide)] = total(zh)
        return carry

    lax.fori_loop(0, tiles, over_y, 0)

    def turn(source, carry):
        left = dot_nt(eye, mix_ref[source].reshape(ch, TOK)).astype(bf16)
        ml_ref[:, pl.ds(pl.multiple_of(source * ch, ch), ch)] = left
        return carry

    lax.fori_loop(0, nt, turn, 0)

    def project(i, carry):
        columns = pl.ds(pl.multiple_of(i * wide, wide), wide)
        out_ref[:, columns] = dot_nn(ml_ref[...], w_ref[:, columns]).astype(bf16)
        return carry

    lax.fori_loop(0, tiles, project, 0)

    def query(j, carry):
        rows = pl.ds(pl.multiple_of(j * TOK, TOK), TOK)
        grad = (gm_ref[rows, :] * yr_ref[rows, :]).astype(bf16)
        gq_ref[:, rows] = dot_nt(eye, grad).astype(bf16)
        return carry

    lax.fori_loop(0, ch // TOK, query, 0)
    leaving = [bring(6, out_ref, outh_ref), bring(7, gq_ref, gqh_ref)]
    wait_rows(pqr_ref, (n - 1) * 2 * OWN, recv_sem.at[3])
    back = pl.ds(pl.multiple_of((n - 1 - me) * 2 * OWN, 2 * OWN), 2 * OWN)
    pqr_ref[mine, :] = pqs_ref[back, :]

    def finish(j, carry):
        lanes = pl.ds(pl.multiple_of(j * TOK, TOK), TOK)
        both = pqr_ref[pl.ds(pl.multiple_of(2 * j * TOK, TOK), 2 * TOK), :].astype(f32)
        both = both.reshape(TOK // OWN, 2 * OWN, TOK)
        grad_gated = dot_nt(rev, both[:, :OWN].reshape(TOK, TOK).astype(bf16))
        gf_ref[:, lanes] = dot_nt(rev, both[:, OWN:].reshape(TOK, TOK).astype(bf16))
        gk_ref[:, lanes] = (grad_gated * v_ref[:, lanes].astype(f32)).astype(bf16)
        gv_ref[:, lanes] = (grad_gated * k_ref[:, lanes].astype(f32)).astype(bf16)
        return carry

    lax.fori_loop(0, ch // TOK, finish, 0)

    leaving += [
        bring(8, gk_ref, gkh_ref),
        bring(9, gv_ref, gvh_ref),
        bring(10, gf_ref, gfh_ref),
    ]

    def over_z(i, carry):
        across(i).wait_recv()
        columns = pl.ds(pl.multiple_of(i * wide, wide), wide)
        gw_ref[:, columns] = gw_ref[:, columns] + zr_ref[i].astype(f32)
        return carry

    lax.fori_loop(0, tiles, over_z, 0)

    leaving.append(bring(11, gw_ref, gwh_ref))

    for copy in leaving:
        copy.wait()
    wait_rows(s1_ref, (n - 1) * 2 * OWN, send_sem.at[0])
    wait_rows(gsb_ref, n - 1, send_sem.at[1])
    wait_rows(ysb_ref, n - 1, send_sem.at[2])
    wait_rows(pqs_ref, (n - 1) * 2 * OWN, send_sem.at[3])
    wait_rows(b_ref, nx - 1, b_send)
    if nc > 1:
        wait_rows(b_ref, nx * (nc - 1), send_sem.at[4])

    wait_rows(a_ref, group - 1, a_send)

    def left_tile(i, carry):
        pltpu.make_async_copy(cs_ref.at[i], cs_ref.at[i], c_send.at[i]).wait()
        across(i).wait_send()
        return carry

    lax.fori_loop(0, tiles, left_tile, 0)
    for step in range(1, nt):
        peer = {"tp": (tp + step) % nt}
        remote(
            ps_ref.at[step - 1],
            pr_ref.at[step - 1],
            tp_send.at[step - 1],
            tp_recv.at[step - 1],
            peer,
        ).wait_send()
    for hop in range(nt - 1):
        for piece in range(2):
            for way in range(2):

                @pl.when(has_next(way) & has_hop(way, hop))
                def _(way=way, hop=hop, piece=piece):
                    pass_on(tp - hop * (1 - 2 * way), way, hop, piece).wait_send()


def place_kernel(*refs):
    copies = [
        pltpu.make_async_copy(refs[i], refs[6 + i], refs[12].at[i]) for i in range(6)
    ]
    for copy in copies:
        copy.start()
    for copy in copies:
        copy.wait()


def place(arrays):
    anywhere = pl.BlockSpec(memory_space=pl.ANY)
    return pl.pallas_call(
        place_kernel,
        out_shape=tuple(jax.ShapeDtypeStruct(a.shape, a.dtype) for a in arrays),
        in_specs=[anywhere] * 6,
        out_specs=[pl.BlockSpec(memory_space=pltpu.VMEM)] * 6,
        scratch_shapes=[pltpu.SemaphoreType.DMA((6,))],
        compiler_params=pltpu.CompilerParams(vmem_limit_bytes=60 * 1024 * 1024),
    )(*arrays)


def per_device(dims, q, k, v, f, w, go):
    nx, ny, nz, nc, nt = dims
    n = nx * ny * nz * nc
    ch = OWN * n
    every = ch * nt
    cols = go.shape[1]
    gwr = every // n
    group = nx * nc
    tall = nz * gwr
    wide = min(cols, 256)
    tiles = cols // wide
    anywhere = pl.BlockSpec(memory_space=pl.ANY)
    results = pl.pallas_call(
        functools.partial(kernel, dims),
        out_shape=(
            jax.ShapeDtypeStruct((TOK, cols), bf16),
            jax.ShapeDtypeStruct((TOK, ch), bf16),
            jax.ShapeDtypeStruct((TOK, ch), bf16),
            jax.ShapeDtypeStruct((TOK, ch), bf16),
            jax.ShapeDtypeStruct((TOK, ch), f32),
            jax.ShapeDtypeStruct((gwr, cols), f32),
        ),
        in_specs=[anywhere] * 6,
        out_specs=[anywhere] * 6,
        scratch_shapes=[
            pltpu.VMEM((TOK, ch), bf16),
            pltpu.VMEM((TOK, ch), bf16),
            pltpu.VMEM((TOK, ch), bf16),
            pltpu.VMEM((TOK, ch), f32),
            pltpu.VMEM((TOK, cols), bf16),
            pltpu.VMEM((TOK, cols), bf16),
            pltpu.VMEM((TOK, ch), bf16),
            pltpu.VMEM((TOK, ch), bf16),
            pltpu.VMEM((TOK, ch), bf16),
            pltpu.VMEM((TOK, ch), f32),
            pltpu.VMEM((gwr, cols), f32),
            pltpu.VMEM((2 * ch, TOK), bf16),
            pltpu.VMEM((2 * ch, TOK), bf16),
            pltpu.VMEM((2 * ch, TOK), f32),
            pltpu.VMEM((OWN, 2 * n, TOK), f32),
            pltpu.VMEM((OWN, 2 * n, TOK), f32),
            pltpu.VMEM((OWN, n, TOK, 2 * TOK), bf16),
            pltpu.VMEM((ch, TOK), f32),
            pltpu.VMEM((ch, TOK), f32),
            pltpu.VMEM((nt - 1, ch, TOK), bf16),
            pltpu.VMEM((nt - 1, ch, TOK), bf16),
            pltpu.VMEM((n, OWN, TOK), bf16),
            pltpu.VMEM((n, OWN, TOK), bf16),
            pltpu.VMEM((ch, TOK), f32),
            pltpu.VMEM((ch, TOK), f32),
            pltpu.VMEM((n, OWN, TOK), bf16),
            pltpu.VMEM((n, OWN, TOK), bf16),
            pltpu.VMEM((ch, TOK), f32),
            pltpu.VMEM((2 * ch, TOK), f32),
            pltpu.VMEM((2 * ch, TOK), bf16),
            pltpu.VMEM((2 * ch, TOK), bf16),
            pltpu.VMEM((nt, ny * nz, nc, gwr, TOK), bf16),
            pltpu.VMEM((TOK, every), bf16),
            pltpu.VMEM((every, cols), bf16),
            pltpu.VMEM((group, TOK, cols), bf16),
            pltpu.VMEM((group, ny * nz, gwr, TOK), bf16),
            pltpu.VMEM((tiles, ny * nz * gwr, wide), f32),
            pltpu.VMEM((tiles, ny - 1, tall, wide), bf16),
            pltpu.VMEM((tiles, ny - 1, tall, wide), bf16),
            pltpu.VMEM((tiles, gwr, wide), bf16),
            pltpu.VMEM((tiles, gwr, wide), bf16),
            pltpu.SemaphoreType.DMA((5,)),
            pltpu.SemaphoreType.DMA((5,)),
            pltpu.SemaphoreType.DMA((nt - 1,)),
            pltpu.SemaphoreType.DMA((nt - 1,)),
            pltpu.SemaphoreType.DMA((2, nt - 1, 2)),
            pltpu.SemaphoreType.DMA((2, nt - 1, 2)),
            pltpu.SemaphoreType.DMA,
            pltpu.SemaphoreType.DMA,
            pltpu.SemaphoreType.DMA,
            pltpu.SemaphoreType.DMA,
            pltpu.SemaphoreType.DMA((tiles,)),
            pltpu.SemaphoreType.DMA((tiles,)),
            pltpu.SemaphoreType.DMA((tiles,)),
            pltpu.SemaphoreType.DMA((tiles,)),
            pltpu.SemaphoreType.DMA((12,)),
        ],
        compiler_params=pltpu.CompilerParams(
            collective_id=0, has_side_effects=True, vmem_limit_bytes=56 * 1024 * 1024
        ),
    )(q, k, v, f, w, go)
    return place(results)


def solution(mesh, dims=(4, 4, 2, 2, 4)):
    return jax.shard_map(
        functools.partial(per_device, dims),
        mesh=mesh,
        in_specs=(
            P("ctx", "tp"),
            P("ctx", "tp"),
            P("ctx", "tp"),
            P("ctx", "tp"),
            P(None, "tp"),
            P("ctx", "tp"),
        ),
        out_specs=(P("ctx", "tp"),) * 6,
        check_vma=False,
    )
```
